512 devices in a mesh: lat: 64 (over z, x), mem: 8 (over y, core).
Axes of the slice: x: 4, y: 4, z: 16, core: 2. Of those that a mesh axis runs over, the one named last changes fastest.
Arguments:
- field: bfloat16 [8, 64, 128, 2688], P('mem', 'lat'), may hold values from -6 to 6
- lon_count: int32 [64], P('lat'), may hold values from 16 to 2688, as said below
- wave_order: int32 [640], replicated, may hold values from 0 to 639, as said below
- legendre: bfloat16 [640, 64, 640], P('lat'), may hold values from -0.75 to 0.75
Outputs:
- covariance: float32 [2, 320, 128, 128], P(None, 'lat', 'mem')
The draws below stay inside these ranges and needn't reach their ends.
Inputs may be any that keep to these rules, and one draw needn't show every extreme that they name: `lon_count`: each row's count is 4 k + 16 for a whole k; longitude slots at or beyond it are not part of the row. `wave_order`: each zonal wavenumber stands in exactly one slot; slots 2 t and 2 t + 1 hold wavenumbers that sum to 639.
All inputs are finite; a program needn't handle non-finite values.
Results may differ from the reference program's by a relative error of at most 0.0033.
Values may be sent and summed in bfloat16 or wider, within the bound.
A program may use at most 64 MiB of HBM per device.

```python
import jax
import jax.numpy as jnp
from jax import lax

LEV = 128
LONS = 2688
M = 640
NLAT = 64
MEMBERS = 8


def draw_lon_count(key, part):
    key = jax.random.fold_in(key, 7)
    key_count, key_place = jax.random.split(key)
    largest = (LONS - 16) // 4
    steps = jax.random.randint(key_count, (NLAT,), 0, largest + 1)
    chosen = jax.random.randint(key_place, (), 0, NLAT)
    steps = jnp.where(jnp.arange(NLAT) == chosen, largest, steps)
    return (4 * steps + 16).astype(jnp.int32)


def draw_wave_order(key, part):
    key = jax.random.fold_in(key, 11)
    key_perm, key_flip = jax.random.split(key)
    half = M // 2
    paired = jax.random.permutation(key_perm, half).astype(jnp.int32)
    flips = jax.random.randint(key_flip, (half,), 0, 2)
    first = jnp.where(flips == 1, paired, M - 1 - paired)
    second = M - 1 - first
    return jnp.stack([first, second], axis=1).reshape(M).astype(jnp.int32)


def shard_levels(rng, dims, cuts, smallest, top_value):
    def one(dim, blocks):
        heights = jax.random.uniform(jax.random.fold_in(jax.random.fold_in(rng, 6), dim), (blocks,), jnp.float32, smallest / len(cuts), top_value / len(cuts))
        return jnp.repeat(jnp.exp(heights), dims[dim] // blocks).reshape((-1,) + (1,) * (len(dims) - dim - 1))

    factor_of = one(*cuts[0])
    for cut in cuts[1:]:
        factor_of = factor_of * one(*cut)
    return factor_of


def scatter_about(stream_key, dims, width, limit, pieces=(), held_as=jnp.bfloat16):
    gain = shard_levels(stream_key, dims, pieces, -0.22, 0.18) if pieces else 1.0
    entries = jax.random.normal(stream_key, dims, jnp.float32) * width * gain
    return jnp.minimum(jnp.maximum(entries, -limit), limit).astype(held_as)


def setup_inputs(seed: int = 0) -> dict:
    key_list = jax.random.split(jax.random.key(seed), 5)
    field = scatter_about(key_list[0], (MEMBERS, NLAT, LEV, LONS), 1.0, 6.0, ((0, 8), (1, 64)))
    lon_count = draw_lon_count(jax.random.fold_in(key_list[4], 71), 0)
    wave_order = draw_wave_order(jax.random.fold_in(key_list[4], 71), 0)
    legendre = scatter_about(key_list[3], (M, NLAT, M), NLAT ** -0.5, 0.75, ((0, 64),))
    return dict(field=field, lon_count=lon_count, wave_order=wave_order, legendre=legendre)


TWO_PI = 6.283185307179586


def build_table(wave_order, count, lons):
    column = lax.iota(jnp.int32, lons)
    product = (wave_order[:, None] * column[None, :]) % count
    angle = product.astype(jnp.float32) * jnp.float32(TWO_PI) / count.astype(jnp.float32)
    inside = (column < count)[None, :]
    real_part = jnp.where(inside, jnp.cos(angle), jnp.float32(0.0))
    imag_part = jnp.where(inside, -jnp.sin(angle), jnp.float32(0.0))
    return jnp.stack([real_part, imag_part], axis=1).astype(jnp.bfloat16)


def reference(field, lon_count, wave_order, legendre):
    members, nlat, levels, lons = field.shape
    waves = wave_order.shape[0]
    total = legendre.shape[2]
    wave_index = lax.iota(jnp.int32, total)
    masked = jnp.where(wave_index[None, None, :] >= wave_order[:, None, None], legendre, jnp.zeros_like(legendre))
    covariance = jnp.zeros((total, levels, levels), jnp.float32)
    for member in range(members):
        def one_row(pair):
            row_data, count = pair
            table = build_table(wave_order, count, lons)
            summed = jnp.einsum('mck,lk->mcl', table.astype(jnp.float32), row_data.astype(jnp.float32))
            return (summed / count.astype(jnp.float32)).astype(jnp.bfloat16).reshape(waves, 2 * levels)
        fourier = lax.map(one_row, (field[member], lon_count))
        fourier = jnp.transpose(fourier, (1, 0, 2))
        spectral = jnp.einsum('srn,srk->snk', masked.astype(jnp.float32), fourier.astype(jnp.float32)).astype(jnp.bfloat16)
        spectral = spectral.reshape(waves, total, 2, levels).astype(jnp.float32)
        covariance = covariance + jnp.einsum('snca,sncb->nab', spectral, spectral)
    covariance = covariance / jnp.float32(members)
    half = total // 2
    return jnp.stack([covariance[:half], jnp.flip(covariance[half:], 0)])
```

```python
import jax
import jax.numpy as jnp
from jax import lax
from jax.experimental import pallas as pl
from jax.experimental.pallas import tpu as pltpu
from jax.sharding import PartitionSpec as P

MESH = pl.DeviceIdType.MESH
F32 = jnp.float32
BF16 = jnp.bfloat16
Z, X, D = 16, 4, 8
GROUP = X * D
LEV, LONS, M = 128, 2688, 640
PAIRS = 5
OWN = 10
COS = (1.0, -19.739208221435547, 64.93939208984375, -85.45681762695312, 60.24457931518555,
       -26.425565719604492, 7.898900985717773, -1.6961979866027832, 0.24304766952991486)
SIN = (6.2831854820251465, -41.34170150756836, 81.6052474975586, -76.70585632324219, 42.05867385864258,
       -15.094411849975586, 3.818404197692871, -0.7120527029037476, 0.09126123040914536)


def iota(shape, dim):
    return lax.broadcasted_iota(jnp.int32, shape, dim)


def dot(a, b, ca, cb):
    return lax.dot_general(a, b, (((ca,), (cb,)), ((), ())), preferred_element_type=F32)


def poly(coefficients, v):
    total = jnp.full_like(v, coefficients[-1])
    for value in coefficients[-2::-1]:
        total = total * v + value
    return total


def unit(product, count, inverse):
    turns = jnp.floor(product * inverse + 0.5)
    u = (product - turns * count) * inverse
    v = u * u
    return poly(COS, v), -u * poly(SIN, v)


def one_hot(condition):
    return jnp.where(condition, 1.0, 0.0).astype(BF16)


def total_wave(dest, k):
    t = (dest & 7) + 8 * k
    zz = (t * 205) >> 10
    return 20 * zz + 5 * (dest >> 3) + (t - 5 * zz)


def kernel(count_ref, wave_ref, waves_ref, field_ref, leg_ref, out_ref,
           fm, tbl, base, zs, zr, xs, xr, p256, prow, pcol, lr, lu, lv, lul, lvl, lw,
           psa, psb, psc, pra, prb, prc, ab, mt, acc, rs, rr, mm,
           zs_sem, zr_sem, xs_sem, xr_sem, ps_sem, pr_sem, rs_sem, rr_sem, ms_sem, mr_sem):
    lat = lax.axis_index("lat")
    d = lax.axis_index("mem")
    z, x = lat // X, lat % X
    me = x * D + d

    def z_partner(o):
        other = (z + o) % Z
        return other, (other * X + x, d)

    def plane_partner(o):
        other = (me + o) % GROUP
        return other, (z * X + other // D, other % D)

    barrier = pltpu.get_barrier_semaphore()

    def greet_z(o, carry):
        pl.semaphore_signal(barrier, inc=1, device_id=z_partner(o)[1], device_id_type=MESH)
        return carry

    def greet_plane(o, carry):
        pl.semaphore_signal(barrier, inc=1, device_id=plane_partner(o)[1], device_id_type=MESH)
        return carry

    lax.fori_loop(1, Z, greet_z, 0)
    lax.fori_loop(1, GROUP, greet_plane, 0)

    count = count_ref[0].astype(F32)
    inverse = 1.0 / jnp.full((128, 128), count, F32)
    fm[...] = jnp.where(iota((LEV, LONS), 1) < count_ref[0], field_ref[...].astype(F32), 0.0).astype(BF16)
    wave_row = waves_ref[...].astype(F32)
    p_row = iota((128, M), 0)

    def make_base(j, carry):
        slot = 10 * (p_row >> 1) + 2 * j + (p_row & 1)
        wave = jnp.sum(jnp.where(iota((128, M), 1) == slot, wave_row, 0.0), axis=1, keepdims=True)
        wave = jnp.broadcast_to(wave, (128, 128))
        c, s = unit(wave * iota((128, 128), 1).astype(F32), count, inverse)
        base[j, 0] = c
        base[j, 1] = s
        c, s = unit(wave * 128.0, count, inverse)
        base[j, 2] = c
        base[j, 3] = s
        return carry

    lax.fori_loop(0, PAIRS, make_base, 0)
    pl.semaphore_wait(barrier, Z - 1 + GROUP - 1)

    def transform(j, carry):
        def rows(b, inner):
            at = pl.ds(pl.multiple_of(b * 32, 32), 32)
            c, s = base[j, 0, at, :], base[j, 1, at, :]
            cw, sw = base[j, 2, at, :], base[j, 3, at, :]
            for a in range(LONS // 128):
                tbl[0, at, a * 128:(a + 1) * 128] = c.astype(BF16)
                tbl[1, at, a * 128:(a + 1) * 128] = s.astype(BF16)
                c, s = c * cw - s * sw, c * sw + s * cw
            return inner

        lax.fori_loop(0, 4, rows, 0)
        summed = dot(tbl[...].reshape(256, LONS), fm[...], 1, 1) / count
        both = summed.reshape(2, Z, 8, LEV)
        zs[j] = jnp.concatenate([both[0], both[1]], axis=1).astype(BF16)
        zr[j, z] = zs[j, z]

        def send(o, inner):
            other, device = z_partner(o)
            pltpu.make_async_remote_copy(
                src_ref=zs.at[j, other], dst_ref=zr.at[j, z], send_sem=zs_sem, recv_sem=zr_sem.at[j],
                device_id=device, device_id_type=MESH).start()
            return inner

        lax.fori_loop(1, Z, send, 0)
        return carry

    lax.fori_loop(0, PAIRS, transform, 0)

    o_row, o_col = iota((256, 256), 0), iota((256, 256), 1)
    p256[...] = one_hot(o_col == (o_row & 15) * 16 + (o_row >> 4))
    o_row, o_col = iota((128, 128), 0), iota((128, 128), 1)
    prow[...] = one_hot(o_col == ((o_row >> 4) & 1) * 64 + 4 * (o_row & 15) + (o_row >> 5))
    c_row = iota((256, 1), 0)
    i_main = total_wave(c_row >> 3, c_row & 7)
    i_left = total_wave(c_row >> 3, 8 + (c_row & 1))
    n_col = iota((256, M), 1)
    pcol[0:256] = one_hot(n_col == M - 1 - i_main)
    pcol[256:512] = one_hot(n_col == i_main)
    pcol[512:768] = one_hot(n_col == M - 1 - i_left)
    pcol[768:1024] = one_hot(n_col == i_left)

    lane_slot = (iota((1, 128), 1) >> 4) & 1
    left_j = (c_row >> 1) & 3

    def legendre(j, carry):
        lr[j] = dot(prow[...], leg_ref[pl.ds(2 * j, 2)].reshape(128, M), 1, 0).astype(BF16)
        w0 = wave_ref[10 * lat + 2 * j]
        w1 = wave_ref[10 * lat + 2 * j + 1]
        low = jnp.minimum(w0, w1)
        small = jnp.where(lane_slot == 0, w0, w1) == low
        put = pcol[...]
        moved = dot(put, lr[j], 1, 1)
        upper, lower, upper_left, lower_left = (moved[a * 256:(a + 1) * 256] for a in range(4))
        lu[j] = jnp.where(small, upper, 0.0).astype(BF16)
        lv[j] = jnp.where(small, jnp.where(i_main >= low, lower, 0.0),
                          jnp.where(i_main < low, upper, 0.0)).astype(BF16)
        here = left_j == lax.rem(j, 4)
        lul[j] = jnp.where(here & small, upper_left, 0.0).astype(BF16)
        lvl[j] = jnp.where(small, jnp.where(here & (i_left >= low), lower_left, 0.0),
                           jnp.where(here & (i_left < low), upper_left, 0.0)).astype(BF16)
        pick = one_hot((iota((16, M), 0) == 2 + j) & (iota((16, M), 1) == M - 1 - low))
        lw[j] = jnp.where(small, 0.0, dot(pick, lr[j], 1, 1)).astype(BF16)
        for xx in range(X):
            wave = wave_ref[10 * (X * z + xx) + 2 * j]
            mt[j, xx * 8:(xx + 1) * 8, :] = jnp.full((8, 128), jnp.minimum(wave, M - 1 - wave), jnp.int32)
        return carry

    lax.fori_loop(0, PAIRS, legendre, 0)

    def swap_rows(j):
        pltpu.make_async_copy(zr.at[j, 0:Z - 1], zr.at[j, 0:Z - 1], zr_sem.at[j]).wait()
        moved = dot(p256[...], zr[j].reshape(256, LEV), 1, 0).astype(BF16)
        for q in range(2):
            for xx in range(X):
                at = (q * 8 + xx * 2) * 16
                xs[j, xx, :, q * 128:(q + 1) * 128] = moved[at:at + 32]
        xr[j, x] = xs[j, x]

        def send(o, carry):
            other = (x + o) % X
            pltpu.make_async_remote_copy(
                src_ref=xs.at[j, other], dst_ref=xr.at[j, x], send_sem=xs_sem, recv_sem=xr_sem.at[j],
                device_id=(z * X + other, d), device_id_type=MESH).start()
            return carry

        lax.fori_loop(1, X, send, 0)

    def rows_in(j):
        pltpu.make_async_copy(xr.at[j, 0:X - 1], xr.at[j, 0:X - 1], xr_sem.at[j]).wait()

    def both_kinds(up, low):
        return jnp.concatenate([up.reshape(GROUP, 8, 256), low.reshape(GROUP, 8, 256)], axis=1).astype(BF16)

    def spectral(j, target, place):
        rhs = xr[j].reshape(128, 256)
        target[:, place:place + 16, :] = both_kinds(dot(lu[j], rhs, 1, 0), dot(lv[j], rhs, 1, 0))

    def send_plane(stage, source, target):
        target[me] = source[me]

        def send(o, carry):
            other, device = plane_partner(o)
            pltpu.make_async_remote_copy(
                src_ref=source.at[other], dst_ref=target.at[me], send_sem=ps_sem.at[stage],
                recv_sem=pr_sem.at[stage], device_id=device, device_id_type=MESH).start()
            return carry

        lax.fori_loop(1, GROUP, send, 0)

    swap_rows(0)
    swap_rows(1)
    rows_in(0)
    spectral(0, psa, 0)
    rows_in(1)
    spectral(1, psa, 16)
    send_plane(0, psa, pra)
    swap_rows(2)
    swap_rows(3)
    rows_in(2)
    spectral(2, psb, 0)
    rows_in(3)
    spectral(3, psb, 16)
    up, low = jnp.zeros((256, 256), F32), jnp.zeros((256, 256), F32)
    for j in range(4):
        rhs = xr[j].reshape(128, 256)
        up += dot(lul[j], rhs, 1, 0)
        low += dot(lvl[j], rhs, 1, 0)
    psb[:, 32:48, :] = both_kinds(up, low)
    send_plane(1, psb, prb)
    swap_rows(4)
    rows_in(4)
    spectral(4, psc, 0)
    rhs = xr[4].reshape(128, 256)
    extra = jnp.zeros((16, 256), F32)
    for j in range(PAIRS):
        extra += dot(lw[j], xr[j].reshape(128, 256), 1, 0)
    up = dot(lul[4], rhs, 1, 0).reshape(GROUP, 8, 256) + extra[0:8][None]
    psc[:, 16:32, :] = both_kinds(up, dot(lvl[4], rhs, 1, 0))
    send_plane(2, psc, prc)

    def arrived(stage, target, subs):
        pltpu.make_async_copy(target.at[0:GROUP - 1], target.at[0:GROUP - 1], pr_sem.at[stage]).wait()
        for b, sub in enumerate(subs):
            for g in range(2):
                piece = target[g * 16:(g + 1) * 16, b * 16:(b + 1) * 16, :].reshape(256, 256)
                moved = dot(p256[...], piece, 1, 0).astype(BF16)
                ab[sub, :, g * 16:(g + 1) * 16, :] = moved.reshape(16, 16, 256)

    def halves(rows):
        return jnp.concatenate([rows[:, 0:128], rows[:, 128:256]], axis=0)

    def waves_of(js):
        tile = jnp.concatenate([mt[j] for j in js], axis=0)
        return jnp.concatenate([tile, tile], axis=0)

    def gram(k, ups, lows, js, first, extras=None):
        i = total_wave(me, k)
        up = halves(jnp.concatenate(ups, axis=0))
        low = halves(jnp.concatenate(lows, axis=0))
        waves = waves_of(js)
        inside = low * one_hot(waves <= i)
        outside = low * one_hot(waves > i)
        near = dot(low, inside, 0, 0)
        far = dot(up, up, 0, 0) + dot(low, outside, 0, 0)
        if extras is not None:
            far += dot(extras, extras * one_hot(waves_of(range(PAIRS)) == i), 0, 0)
        if first:
            acc[k, 0] = near
            acc[k, 1] = far
        else:
            acc[k, 0] += near
            acc[k, 1] += far

    arrived(0, pra, (0, 1))

    def gram_a(k, carry):
        gram(k, [ab[0, k], ab[1, k]], [ab[0, 8 + k], ab[1, 8 + k]], (0, 1), True)
        return carry

    lax.fori_loop(0, 8, gram_a, 0)
    arrived(1, prb, (2, 3, 5))

    def gram_b(k, carry):
        gram(k, [ab[2, k], ab[3, k]], [ab[2, 8 + k], ab[3, 8 + k]], (2, 3), False)
        return carry

    lax.fori_loop(0, 8, gram_b, 0)
    for kk in range(2):
        gram(8 + kk, [ab[5, 2 * j + kk] for j in range(4)], [ab[5, 8 + 2 * j + kk] for j in range(4)],
             (0, 1, 2, 3), True)
    arrived(2, prc, (4, 6))
    extras = halves(jnp.concatenate([ab[6, 2 + j] for j in range(PAIRS)], axis=0))

    lane = iota((16, 128), 1)

    def pack_send(k):
        for h in range(2):
            whole = acc[k, h]
            blocks = [whole[0:16]]
            for r in range(1, 4):
                folded = pltpu.roll(whole[16 * (8 - r):16 * (9 - r)], 16 * r, 1)
                blocks.append(jnp.where(lane >= 16 * r, whole[16 * r:16 * (r + 1)], folded))
            blocks.append(whole[64:80])
            rs[k, h * 80:(h + 1) * 80, :] = jnp.concatenate(blocks, axis=0).astype(BF16)
        owner = (d + 8 * k) // 5

        @pl.when(owner == z)
        def _():
            rr[z] = rs[k]

        @pl.when(owner != z)
        def _():
            pltpu.make_async_remote_copy(
                src_ref=rs.at[k], dst_ref=rr.at[z], send_sem=rs_sem, recv_sem=rr_sem,
                device_id=(owner * X + x, d), device_id_type=MESH).start()

    def gram_c(k, carry):
        gram(k, [ab[4, k]], [ab[4, 8 + k]], (4,), False, extras)
        pack_send(k)
        return carry

    lax.fori_loop(0, 8, gram_c, 0)

    def gram_d(kk, carry):
        gram(8 + kk, [ab[6, kk]], [ab[6, 8 + kk]], (4,), False, extras)
        pack_send(8 + kk)
        return carry

    lax.fori_loop(0, 2, gram_d, 0)

    u = (d + 3 * z) % 8
    holds = u < 5

    @pl.when(holds)
    def _():
        pltpu.make_async_copy(rr.at[0:Z - 1], rr.at[0:Z - 1], rr_sem).wait()
        total = rr[0].astype(F32)
        for a in range(1, Z):
            total += rr[a].astype(F32)
        total = total * 0.125
        for h in range(2):
            part = total[h * 80:(h + 1) * 80]
            blocks = [part[16 * r:16 * (r + 1)] for r in range(5)]
            for r in range(3, 0, -1):
                blocks.append(pltpu.roll(part[16 * r:16 * (r + 1)], 128 - 16 * r, 1))
            upper = jnp.concatenate(blocks, axis=0)
            keep = (iota((128, 128), 1) >> 4) >= (iota((128, 128), 0) >> 4)
            full = jnp.where(keep, upper, upper.T)
            mm[:, h] = full.reshape(8, 16, 128)
        out_ref[:, u] = mm[d]

        def send(o, carry):
            other = (d + o) % D
            pltpu.make_async_remote_copy(
                src_ref=mm.at[other], dst_ref=out_ref.at[:, u], send_sem=ms_sem, recv_sem=mr_sem,
                device_id=(lat, other), device_id_type=MESH).start()
            return carry

        lax.fori_loop(1, D, send, 0)

    @pl.when(holds)
    def _():
        pltpu.make_async_copy(out_ref.at[:, 0:4], out_ref.at[:, 0:4], mr_sem).wait()
        pltpu.make_async_copy(mm.at[0:7], mm.at[0:7], ms_sem).wait()

    @pl.when(jnp.logical_not(holds))
    def _():
        pltpu.make_async_copy(out_ref, out_ref, mr_sem).wait()

    for j in range(PAIRS):
        pltpu.make_async_copy(zs.at[j, 0:Z - 1], zs.at[j, 0:Z - 1], zs_sem).wait()
        pltpu.make_async_copy(xs.at[j, 0:X - 1], xs.at[j, 0:X - 1], xs_sem).wait()
    for stage, source in enumerate((psa, psb, psc)):
        pltpu.make_async_copy(source.at[0:GROUP - 1], source.at[0:GROUP - 1], ps_sem.at[stage]).wait()

    @pl.when(holds)
    def _():
        pltpu.make_async_copy(rs.at[0:OWN - 1], rs.at[0:OWN - 1], rs_sem).wait()

    @pl.when(jnp.logical_not(holds))
    def _():
        pltpu.make_async_copy(rs, rs, rs_sem).wait()


def per_device(field, lon_count, wave_order, legendre):
    vmem = pl.BlockSpec(memory_space=pltpu.VMEM)
    smem = pl.BlockSpec(memory_space=pltpu.SMEM)
    V = pltpu.VMEM
    scratch = [
        V((LEV, LONS), BF16), V((2, 128, LONS), BF16), V((PAIRS, 4, 128, 128), F32),
        V((PAIRS, Z, 16, LEV), BF16), V((PAIRS, Z, 16, LEV), BF16),
        V((PAIRS, X, 32, 256), BF16), V((PAIRS, X, 32, 256), BF16),
        V((256, 256), BF16), V((128, 128), BF16), V((1024, M), BF16), V((PAIRS, 128, M), BF16),
        V((PAIRS, 256, 128), BF16), V((PAIRS, 256, 128), BF16),
        V((PAIRS, 256, 128), BF16), V((PAIRS, 256, 128), BF16), V((PAIRS, 16, 128), BF16),
        V((GROUP, 32, 256), BF16), V((GROUP, 48, 256), BF16), V((GROUP, 32, 256), BF16),
        V((GROUP, 32, 256), BF16), V((GROUP, 48, 256), BF16), V((GROUP, 32, 256), BF16),
        V((7, 16, GROUP, 256), BF16), V((PAIRS, 32, 128), jnp.int32), V((OWN, 2, 128, 128), F32),
        V((OWN, 160, 128), BF16), V((Z, 160, 128), BF16), V((D, 2, 16, 128), F32),
        pltpu.SemaphoreType.DMA, pltpu.SemaphoreType.DMA((PAIRS,)),
        pltpu.SemaphoreType.DMA, pltpu.SemaphoreType.DMA((PAIRS,)),
        pltpu.SemaphoreType.DMA((3,)), pltpu.SemaphoreType.DMA((3,)),
        pltpu.SemaphoreType.DMA, pltpu.SemaphoreType.DMA,
        pltpu.SemaphoreType.DMA, pltpu.SemaphoreType.DMA,
    ]
    return pl.pallas_call(
        kernel,
        out_shape=jax.ShapeDtypeStruct((2, 5, 16, 128), F32),
        in_specs=[smem, smem, vmem, vmem, vmem],
        out_specs=vmem,
        scratch_shapes=scratch,
        compiler_params=pltpu.CompilerParams(
            collective_id=0, has_side_effects=True, vmem_limit_bytes=48 * 1024 * 1024),
    )(lon_count, wave_order, wave_order.reshape(1, M), field.reshape(LEV, LONS), legendre)


def solution(mesh):
    return jax.shard_map(
        per_device,
        mesh=mesh,
        in_specs=(P("mem", "lat", None, None), P("lat"), P(), P("lat", None, None)),
        out_specs=P(None, "lat", "mem", None),
        check_vma=False,
    )
```

```python
import jax
import jax.numpy as jnp
from jax import lax
from jax.experimental import pallas as pl
from jax.experimental.pallas import tpu as pltpu
from jax.sharding import PartitionSpec as P

MESH = pl.DeviceIdType.MESH
F32 = jnp.float32
BF16 = jnp.bfloat16
Z, X, D = 16, 4, 8
GROUP = X * D
LEV, LONS, M, NLAT = 128, 2688, 640, 64
PAIRS = 5
EXTRA = (6, 7, 14, 4, 5)
OWN = 10
COS = (1.0, -19.739208221435547, 64.93939208984375, -85.45681762695312, 60.24457931518555,
       -26.425565719604492, 7.898900985717773, -1.6961979866027832, 0.24304766952991486)
SIN = (6.2831854820251465, -41.34170150756836, 81.6052474975586, -76.70585632324219, 42.05867385864258,
       -15.094411849975586, 3.818404197692871, -0.7120527029037476, 0.09126123040914536)


def iota(shape, dim):
    return lax.broadcasted_iota(jnp.int32, shape, dim)


def dot(a, b, ca, cb):
    return lax.dot_general(a, b, (((ca,), (cb,)), ((), ())), preferred_element_type=F32)


def poly(coefficients, v):
    total = jnp.full_like(v, coefficients[-1])
    for value in coefficients[-2::-1]:
        total = total * v + value
    return total


def unit(product, count, inverse):
    turns = jnp.floor(product * inverse + 0.5)
    u = (product - turns * count) * inverse
    v = u * u
    return poly(COS, v), -u * poly(SIN, v)


def one_hot(condition):
    return jnp.where(condition, 1.0, 0.0).astype(BF16)


def total_wave(dest, k):
    t = (dest & 7) + 8 * k
    zz = (t * 205) >> 10
    return 20 * zz + 5 * (dest >> 3) + (t - 5 * zz)


def kernel(count_ref, wave_ref, waves_ref, field_ref, leg_ref, out_ref,
           fi, li, fm, tbl, base, zsa, zsb, zsc, zra, zrb, zrc, xs, xr, p256, prow, pcol, lr, lu, lv, lul, lvl, lw,
           psa, psb, psc, pra, prb, prc, ab, mt, acc, rs, r1, r2s, r2, mm,
           in_sem, zs_sem, zr_sem, xs_sem, xr_sem, ps_sem, pr_sem, r1s_sem, r1_sem, r2s_sem, r2_sem, ms_sem, mr_sem):
    field_in = pltpu.make_async_copy(field_ref, fi, in_sem.at[0])
    leg_in = pltpu.make_async_copy(leg_ref, li, in_sem.at[1])
    field_in.start()
    leg_in.start()
    lat = lax.axis_index("lat")
    d = lax.axis_index("mem")
    z, x = lat // X, lat % X
    me = x * D + d

    def z_partner(o):
        far = 8 - (o + 1) // 2
        other = (z + far + (1 - o % 2) * (Z - 2 * far)) % Z
        return other, (other * X + x, d)

    def plane_partner(o):
        other = (me + 11 * o) % GROUP
        return other, (z * X + other // D, other % D)

    barrier = pltpu.get_barrier_semaphore()

    def greet_z(o, carry):
        pl.semaphore_signal(barrier, inc=1, device_id=z_partner(o)[1], device_id_type=MESH)
        return carry

    def greet_plane(o, carry):
        pl.semaphore_signal(barrier, inc=1, device_id=plane_partner(o)[1], device_id_type=MESH)
        return carry

    lax.fori_loop(0, Z - 1, greet_z, 0)
    lax.fori_loop(1, GROUP, greet_plane, 0)

    count = count_ref[0].astype(F32)
    inverse = 1.0 / jnp.full((128, 128), count, F32)
    wave_row = waves_ref[...].astype(F32).reshape(1, M)
    p_row = iota((128, M), 0)

    def make_base(j, carry):
        slot = 10 * (p_row >> 1) + 2 * j + (p_row & 1)
        wave = jnp.sum(jnp.where(iota((128, M), 1) == slot, wave_row, 0.0), axis=1, keepdims=True)
        wave = jnp.broadcast_to(wave, (128, 128))
        c, s = unit(wave * iota((128, 128), 1).astype(F32), count, inverse)
        base[j, 0] = c
        base[j, 1] = s
        c, s = unit(wave * 128.0, count, inverse)
        base[j, 2] = c
        base[j, 3] = s
        return carry

    lax.fori_loop(0, PAIRS, make_base, 0)
    field_in.wait()
    fm[...] = jnp.where(iota((LEV, LONS), 1) < count_ref[0], fi[...].astype(F32), 0.0).astype(BF16)

    def transform(j, target, place):
        def rows(b, inner):
            at = pl.ds(pl.multiple_of(b * 32, 32), 32)
            c, s = base[j, 0, at, :], base[j, 1, at, :]
            cw, sw = base[j, 2, at, :], base[j, 3, at, :]
            for a in range(LONS // 128):
                tbl[0, at, a * 128:(a + 1) * 128] = c.astype(BF16)
                tbl[1, at, a * 128:(a + 1) * 128] = s.astype(BF16)
                c, s = c * cw - s * sw, c * sw + s * cw
            return inner

        lax.fori_loop(0, 4, rows, 0)
        summed = dot(tbl[...].reshape(256, LONS), fm[...], 1, 1) / count
        both = summed.reshape(2, Z, 8, LEV)
        target[:, place * 16:place * 16 + 16, :] = jnp.concatenate([both[0], both[1]], axis=1).astype(BF16)

    def send_z(stage, source, target):
        target[z] = source[z]

        def send(o, carry):
            other, device = z_partner(o)
            pltpu.make_async_remote_copy(
                src_ref=source.at[other], dst_ref=target.at[z], send_sem=zs_sem.at[stage],
                recv_sem=zr_sem.at[stage], device_id=device, device_id_type=MESH).start()
            return carry

        lax.fori_loop(0, Z - 1, send, 0)

    transform(0, zsa, 0)
    pl.semaphore_wait(barrier, Z - 1 + GROUP - 1)
    send_z(0, zsa, zra)
    transform(1, zsb, 0)
    transform(2, zsb, 1)
    send_z(1, zsb, zrb)
    transform(3, zsc, 0)
    transform(4, zsc, 1)
    send_z(2, zsc, zrc)

    o_row, o_col = iota((256, 256), 0), iota((256, 256), 1)
    p256[...] = one_hot(o_col == (o_row & 15) * 16 + (o_row >> 4))
    o_row, o_col = iota((128, 128), 0), iota((128, 128), 1)
    prow[...] = one_hot(o_col == ((o_row >> 4) & 1) * 64 + 4 * (o_row & 15) + (o_row >> 5))
    c_row = iota((256, 1), 0)
    i_main = total_wave(c_row >> 3, c_row & 7)
    i_left = total_wave(c_row >> 3, 8 + (c_row & 1))
    n_col = iota((256, M), 1)
    pcol[0:256] = one_hot(n_col == M - 1 - i_main)
    pcol[256:512] = one_hot(n_col == i_main)
    pcol[512:768] = one_hot(n_col == M - 1 - i_left)
    pcol[768:1024] = one_hot(n_col == i_left)

    lane_slot = (iota((1, 128), 1) >> 4) & 1
    left_j = (c_row >> 1) & 3

    def legendre(j):
        lr[j] = dot(prow[...], li[2 * j:2 * j + 2].reshape(128, M), 1, 0).astype(BF16)
        w0 = wave_ref[10 * lat + 2 * j]
        w1 = wave_ref[10 * lat + 2 * j + 1]
        low = jnp.minimum(w0, w1)
        small = jnp.where(lane_slot == 0, w0, w1) == low
        put = pcol[...]
        moved = dot(put, lr[j], 1, 1)
        upper, lower, upper_left, lower_left = (moved[a * 256:(a + 1) * 256] for a in range(4))
        lu[j] = jnp.where(small, upper, 0.0).astype(BF16)
        lv[j] = jnp.where(small, jnp.where(i_main >= low, lower, 0.0),
                          jnp.where(i_main < low, upper, 0.0)).astype(BF16)
        here = left_j == j % 3
        lul[j] = jnp.where(here & small, upper_left, 0.0).astype(BF16)
        lvl[j] = jnp.where(small, jnp.where(here & (i_left >= low), lower_left, 0.0),
                           jnp.where(here & (i_left < low), upper_left, 0.0)).astype(BF16)
        pick = one_hot((iota((16, M), 0) == EXTRA[j]) & (iota((16, M), 1) == M - 1 - low))
        lw[j] = jnp.where(small, 0.0, dot(pick, lr[j], 1, 1)).astype(BF16)
        for xx in range(X):
            wave = wave_ref[10 * (X * z + xx) + 2 * j]
            mt[j, xx * 8:(xx + 1) * 8, :] = jnp.full((8, 128), jnp.minimum(wave, M - 1 - wave), jnp.int32)

    def rows_along_z(stage, source):
        pltpu.make_async_copy(source.at[0:Z - 1], source.at[0:Z - 1], zr_sem.at[stage]).wait()

    def swap_rows(j, source, place):
        piece = source[:, place * 16:place * 16 + 16, :].reshape(256, LEV)
        moved = dot(p256[...], piece, 1, 0).astype(BF16)
        for q in range(2):
            for xx in range(X):
                at = (q * 8 + xx * 2) * 16
                xs[j, xx, :, q * 128:(q + 1) * 128] = moved[at:at + 32]
        xr[j, x] = xs[j, x]

        def send(o, carry):
            other = (x + o) % X
            pltpu.make_async_remote_copy(
                src_ref=xs.at[j, other], dst_ref=xr.at[j, x], send_sem=xs_sem, recv_sem=xr_sem.at[j],
                device_id=(z * X + other, d), device_id_type=MESH).start()
            return carry

        lax.fori_loop(1, X, send, 0)

    def rows_in(j):
        pltpu.make_async_copy(xr.at[j, 0:X - 1], xr.at[j, 0:X - 1], xr_sem.at[j]).wait()

    def both_kinds(up, low):
        return jnp.concatenate([up.reshape(GROUP, 8, 256), low.reshape(GROUP, 8, 256)], axis=1).astype(BF16)

    def spectral(j, target, place):
        rhs = xr[j].reshape(128, 256)
        target[:, place:place + 16, :] = both_kinds(dot(lu[j], rhs, 1, 0), dot(lv[j], rhs, 1, 0))

    def send_plane(stage, source, target):
        target[me] = source[me]

        def send(o, carry):
            other, device = plane_partner(o)
            pltpu.make_async_remote_copy(
                src_ref=source.at[other], dst_ref=target.at[me], send_sem=ps_sem.at[stage],
                recv_sem=pr_sem.at[stage], device_id=device, device_id_type=MESH).start()
            return carry

        lax.fori_loop(1, GROUP, send, 0)

    def left_over(js, target, place):
        up, low = jnp.zeros((256, 256), F32), jnp.zeros((256, 256), F32)
        extra = jnp.zeros((16, 256), F32)
        for j in js:
            rhs = xr[j].reshape(128, 256)
            up += dot(lul[j], rhs, 1, 0)
            low += dot(lvl[j], rhs, 1, 0)
            extra += dot(lw[j], rhs, 1, 0)
        up = up.reshape(GROUP, 8, 256) + extra[0:8][None]
        low = low.reshape(GROUP, 8, 256) + extra[8:16][None]
        target[:, place:place + 16, :] = both_kinds(up, low)

    leg_in.wait()
    legendre(0)
    rows_along_z(0, zra)
    swap_rows(0, zra, 0)
    legendre(1)
    rows_in(0)
    spectral(0, psa, 0)
    send_plane(0, psa, pra)
    legendre(2)
    rows_along_z(1, zrb)
    swap_rows(1, zrb, 0)
    swap_rows(2, zrb, 1)
    legendre(3)
    rows_in(1)
    spectral(1, psb, 0)
    rows_in(2)
    spectral(2, psb, 16)
    left_over((0, 1, 2), psb, 32)
    send_plane(1, psb, prb)
    legendre(4)
    rows_along_z(2, zrc)
    swap_rows(3, zrc, 0)
    swap_rows(4, zrc, 1)
    rows_in(3)
    spectral(3, psc, 0)
    rows_in(4)
    spectral(4, psc, 16)
    left_over((3, 4), psc, 32)
    send_plane(2, psc, prc)

    def arrived(stage, target, subs):
        pltpu.make_async_copy(target.at[0:GROUP - 1], target.at[0:GROUP - 1], pr_sem.at[stage]).wait()
        for b, sub in enumerate(subs):
            for g in range(2):
                piece = target[g * 16:(g + 1) * 16, b * 16:(b + 1) * 16, :].reshape(256, 256)
                moved = dot(p256[...], piece, 1, 0).astype(BF16)
                ab[sub, :, g * 16:(g + 1) * 16, :] = moved.reshape(16, 16, 256)

    def halves(rows):
        return jnp.concatenate([rows[:, 0:128], rows[:, 128:256]], axis=0)

    def waves_of(js):
        tile = jnp.concatenate([mt[j] for j in js], axis=0)
        return jnp.concatenate([tile, tile], axis=0)

    def gram(k, ups, lows, js, first, extras=None, extra_js=()):
        i = total_wave(me, k)
        up = halves(jnp.concatenate(ups, axis=0))
        low = halves(jnp.concatenate(lows, axis=0))
        waves = waves_of(js)
        inside = low * one_hot(waves <= i)
        outside = low * one_hot(waves > i)
        near = dot(low, inside, 0, 0)
        far = dot(up, up, 0, 0) + dot(low, outside, 0, 0)
        if extras is not None:
            far += dot(extras, extras * one_hot(waves_of(extra_js) == i), 0, 0)
        if first:
            acc[k, 0] = near
            acc[k, 1] = far
        else:
            acc[k, 0] += near
            acc[k, 1] += far

    arrived(0, pra, (0,))

    def gram_a(k, carry):
        gram(k, [ab[0, k]], [ab[0, 8 + k]], (0,), True)
        return carry

    lax.fori_loop(0, 8, gram_a, 0)
    arrived(1, prb, (1, 2, 5))
    extras_b = halves(jnp.concatenate([ab[5, EXTRA[j]] for j in (0, 1, 2)], axis=0))

    def gram_b(k, carry):
        gram(k, [ab[1, k], ab[2, k]], [ab[1, 8 + k], ab[2, 8 + k]], (1, 2), False, extras_b, (0, 1, 2))
        return carry

    lax.fori_loop(0, 8, gram_b, 0)
    for kk in range(2):
        gram(8 + kk, [ab[5, 2 * j + kk] for j in range(3)], [ab[5, 8 + 2 * j + kk] for j in range(3)],
             (0, 1, 2), True, extras_b, (0, 1, 2))
    arrived(2, prc, (3, 4, 6))
    extras_c = halves(jnp.concatenate([ab[6, EXTRA[j]] for j in (3, 4)], axis=0))

    lane = iota((16, 128), 1)

    behind = 1 + d % 2

    def owner_of(k):
        return (d + 8 * k) // 5

    def toward(k):
        return (owner_of(k) - z + Z + behind) % 4 - behind

    def pack_send(k):
        for h in range(2):
            whole = acc[k, h]
            blocks = [whole[0:16]]
            for r in range(1, 4):
                folded = pltpu.roll(whole[16 * (8 - r):16 * (9 - r)], 16 * r, 1)
                blocks.append(jnp.where(lane >= 16 * r, whole[16 * r:16 * (r + 1)], folded))
            blocks.append(whole[64:80])
            rs[k, h * 80:(h + 1) * 80, :] = jnp.concatenate(blocks, axis=0).astype(BF16)
        step = toward(k)
        seat = step + behind

        @pl.when(step != 0)
        def _():
            pltpu.make_async_remote_copy(
                src_ref=rs.at[k], dst_ref=r1.at[k, seat - (seat + 3 - behind) // 4], send_sem=r1s_sem,
                recv_sem=r1_sem.at[k], device_id=(((z + step + Z) % Z) * X + x, d), device_id_type=MESH).start()

    def gram_c(k, carry):
        gram(k, [ab[3, k], ab[4, k]], [ab[3, 8 + k], ab[4, 8 + k]], (3, 4), False, extras_c, (3, 4))
        pack_send(k)
        return carry

    def gram_d(kk, carry):
        gram(8 + kk, [ab[6, kk], ab[6, 2 + kk]], [ab[6, 8 + kk], ab[6, 10 + kk]], (3, 4), False, extras_c, (3, 4))
        pack_send(8 + kk)
        return carry

    lax.fori_loop(0, 8, gram_c, 0)
    lax.fori_loop(0, 2, gram_d, 0)

    def level_two(k, carry):
        @pl.when(toward(k) == 0)
        def _():
            pltpu.make_async_copy(r1.at[k], r1.at[k], r1_sem.at[k]).wait()
            total = rs[k].astype(F32)
            for a in range(3):
                total += r1[k, a].astype(F32)
            r2s[k] = total.astype(BF16)
            owner = owner_of(k)

            @pl.when(owner == z)
            def _():
                r2[z // 4] = r2s[k]

            @pl.when(owner != z)
            def _():
                pltpu.make_async_remote_copy(
                    src_ref=r2s.at[k], dst_ref=r2.at[z // 4], send_sem=r2s_sem, recv_sem=r2_sem,
                    device_id=(owner * X + x, d), device_id_type=MESH).start()

        return carry

    lax.fori_loop(0, OWN, level_two, 0)

    u = (d + 3 * z) % 8
    holds = u < 5

    @pl.when(holds)
    def _():
        pltpu.make_async_copy(r2.at[0:3], r2.at[0:3], r2_sem).wait()
        total = r2[0].astype(F32)
        for a in range(1, 4):
            total += r2[a].astype(F32)
        total = total * 0.125
        for h in range(2):
            part = total[h * 80:(h + 1) * 80]
            blocks = [part[16 * r:16 * (r + 1)] for r in range(5)]
            for r in range(3, 0, -1):
                blocks.append(pltpu.roll(part[16 * r:16 * (r + 1)], 128 - 16 * r, 1))
            upper = jnp.concatenate(blocks, axis=0)
            keep = (iota((128, 128), 1) >> 4) >= (iota((128, 128), 0) >> 4)
            full = jnp.where(keep, upper, upper.T)
            mm[:, h] = full.reshape(8, 16, 128)
        out_ref[:, u] = mm[d]

        def send(o, carry):
            other = (d + o) % D
            pltpu.make_async_remote_copy(
                src_ref=mm.at[other], dst_ref=out_ref.at[:, u], send_sem=ms_sem, recv_sem=mr_sem,
                device_id=(lat, other), device_id_type=MESH).start()
            return carry

        lax.fori_loop(1, D, send, 0)

    @pl.when(holds)
    def _():
        pltpu.make_async_copy(out_ref.at[:, 0:4], out_ref.at[:, 0:4], mr_sem).wait()
        pltpu.make_async_copy(mm.at[0:7], mm.at[0:7], ms_sem).wait()

    @pl.when(jnp.logical_not(holds))
    def _():
        pltpu.make_async_copy(out_ref, out_ref, mr_sem).wait()

    for stage, source in enumerate((zsa, zsb, zsc)):
        pltpu.make_async_copy(source.at[0:Z - 1], source.at[0:Z - 1], zs_sem.at[stage]).wait()
    for j in range(PAIRS):
        pltpu.make_async_copy(xs.at[j, 0:X - 1], xs.at[j, 0:X - 1], xs_sem).wait()
    for stage, source in enumerate((psa, psb, psc)):
        pltpu.make_async_copy(source.at[0:GROUP - 1], source.at[0:GROUP - 1], ps_sem.at[stage]).wait()

    def sent(k, carry):
        @pl.when(toward(k) != 0)
        def _():
            pltpu.make_async_copy(rs.at[k], rs.at[k], r1s_sem).wait()

        @pl.when((toward(k) == 0) & (owner_of(k) != z))
        def _():
            pltpu.make_async_copy(r2s.at[k], r2s.at[k], r2s_sem).wait()

        return carry

    lax.fori_loop(0, OWN, sent, 0)


def per_device(field, lon_count, wave_order, legendre):
    vmem = pl.BlockSpec(memory_space=pltpu.VMEM)
    smem = pl.BlockSpec(memory_space=pltpu.SMEM)
    V = pltpu.VMEM
    scratch = [
        V((LEV, LONS), BF16), V((2 * PAIRS, NLAT, M), BF16),
        V((LEV, LONS), BF16), V((2, 128, LONS), BF16), V((PAIRS, 4, 128, 128), F32),
        V((Z, 16, LEV), BF16), V((Z, 32, LEV), BF16), V((Z, 32, LEV), BF16),
        V((Z, 16, LEV), BF16), V((Z, 32, LEV), BF16), V((Z, 32, LEV), BF16),
        V((PAIRS, X, 32, 256), BF16), V((PAIRS, X, 32, 256), BF16),
        V((256, 256), BF16), V((128, 128), BF16), V((1024, M), BF16), V((PAIRS, 128, M), BF16),
        V((PAIRS, 256, 128), BF16), V((PAIRS, 256, 128), BF16),
        V((PAIRS, 256, 128), BF16), V((PAIRS, 256, 128), BF16), V((PAIRS, 16, 128), BF16),
        V((GROUP, 16, 256), BF16), V((GROUP, 48, 256), BF16), V((GROUP, 48, 256), BF16),
        V((GROUP, 16, 256), BF16), V((GROUP, 48, 256), BF16), V((GROUP, 48, 256), BF16),
        V((7, 16, GROUP, 256), BF16), V((PAIRS, 32, 128), jnp.int32), V((OWN, 2, 128, 128), F32),
        V((OWN, 160, 128), BF16), V((OWN, 3, 160, 128), BF16), V((OWN, 160, 128), BF16),
        V((4, 160, 128), BF16), V((D, 2, 16, 128), F32),
        pltpu.SemaphoreType.DMA((2,)),
        pltpu.SemaphoreType.DMA((3,)), pltpu.SemaphoreType.DMA((3,)),
        pltpu.SemaphoreType.DMA, pltpu.SemaphoreType.DMA((PAIRS,)),
        pltpu.SemaphoreType.DMA((3,)), pltpu.SemaphoreType.DMA((3,)),
        pltpu.SemaphoreType.DMA, pltpu.SemaphoreType.DMA((OWN,)),
        pltpu.SemaphoreType.DMA, pltpu.SemaphoreType.DMA,
        pltpu.SemaphoreType.DMA, pltpu.SemaphoreType.DMA,
    ]
    hbm = pl.BlockSpec(memory_space=pl.ANY)
    return pl.pallas_call(
        kernel,
        out_shape=jax.ShapeDtypeStruct((2, 5, 16, 128), F32),
        in_specs=[smem, smem, vmem, hbm, hbm],
        out_specs=vmem,
        scratch_shapes=scratch,
        compiler_params=pltpu.CompilerParams(
            collective_id=0, has_side_effects=True, vmem_limit_bytes=48 * 1024 * 1024),
    )(lon_count, wave_order, wave_order, field.reshape(LEV, LONS), legendre)


def solution(mesh):
    return jax.shard_map(
        per_device,
        mesh=mesh,
        in_specs=(P("mem", "lat", None, None), P("lat"), P(), P("lat", None, None)),
        out_specs=P(None, "lat", "mem", None),
        check_vma=False,
    )
```

```python
import jax
import jax.numpy as jnp
from jax import lax
from jax.experimental import pallas as pl
from jax.experimental.pallas import tpu as pltpu
from jax.sharding import PartitionSpec as P

MESH = pl.DeviceIdType.MESH
F32 = jnp.float32
BF16 = jnp.bfloat16
Z, X, D = 16, 4, 8
GROUP = X * D
LEV, LONS, M, NLAT = 128, 2688, 640, 64
PAIRS = 5
EXTRA = (6, 7, 14, 4, 5)
OWN = 10
COS = (1.0, -19.739208221435547, 64.93939208984375, -85.45681762695312, 60.24457931518555,
       -26.425565719604492, 7.898900985717773, -1.6961979866027832, 0.24304766952991486)
SIN = (6.2831854820251465, -41.34170150756836, 81.6052474975586, -76.70585632324219, 42.05867385864258,
       -15.094411849975586, 3.818404197692871, -0.7120527029037476, 0.09126123040914536)


STEPS = sorted(((dx, dy, dc) for dx in range(4) for dy in range(4) for dc in range(2) if dx or dy or dc),
               key=lambda s: -min(s[0], 4 - s[0]) - min(s[1], 4 - s[1]))


def iota(shape, dim):
    return lax.broadcasted_iota(jnp.int32, shape, dim)


def dot(a, b, ca, cb):
    return lax.dot_general(a, b, (((ca,), (cb,)), ((), ())), preferred_element_type=F32)


def poly(coefficients, v):
    total = jnp.full_like(v, coefficients[-1])
    for value in coefficients[-2::-1]:
        total = total * v + value
    return total


def unit(product, count, inverse):
    turns = jnp.floor(product * inverse + 0.5)
    u = (product - turns * count) * inverse
    v = u * u
    return poly(COS, v), -u * poly(SIN, v)


def one_hot(condition):
    return jnp.where(condition, 1.0, 0.0).astype(BF16)


def total_wave(dest, k):
    t = (dest & 7) + 8 * k
    zz = (t * 205) >> 10
    return 20 * zz + 5 * (dest >> 3) + (t - 5 * zz)


def kernel(count_ref, wave_ref, waves_ref, field_ref, leg_ref, out_ref,
           fi, li, fm, tbl, base, xs, xg, zs0, zs1, zs2, zs3, zr0, zr1, zr2, zr3, xr, p256, pz, prow, pcol, lr, lu, lv, lul, lvl, lw,
           ps0, ps1, ps2, ps3, ps4, ps5, pr0, pr1, pr2, pr3, pr4, pr5, ab, mt, acc, rs, r1, r2s, r2,
           in_sem, zs_sem, zr_sem, xs_sem, xr_sem, ps_sem, pr_sem, r1s_sem, r1_sem, r2s_sem, r2_sem):
    field_in = pltpu.make_async_copy(field_ref, fi, in_sem.at[0])
    leg_in = pltpu.make_async_copy(leg_ref, li, in_sem.at[1])
    field_in.start()
    leg_in.start()
    lat = lax.axis_index("lat")
    d = lax.axis_index("mem")
    z, x = lat // X, lat % X
    me = x * D + d

    def z_partner(o):
        far = 8 - (o + 1) // 2
        other = (z + far + (1 - o % 2) * (Z - 2 * far)) % Z
        return other, (other * X + x, d)

    def plane_partner(step):
        other_x = (x + step[0]) % X
        other_d = (d // 2 + step[1]) % 4 * 2 + (d + step[2]) % 2
        return other_x * D + other_d, (z * X + other_x, other_d)

    barrier = pltpu.get_barrier_semaphore()

    def greet_z(o, carry):
        pl.semaphore_signal(barrier, inc=1, device_id=z_partner(o)[1], device_id_type=MESH)
        return carry

    lax.fori_loop(0, Z - 1, greet_z, 0)
    for step in STEPS:
        pl.semaphore_signal(barrier, inc=1, device_id=plane_partner(step)[1], device_id_type=MESH)

    count = count_ref[0].astype(F32)
    inverse = 1.0 / jnp.full((128, 128), count, F32)
    wave_row = waves_ref[...].astype(F32).reshape(1, M)
    p_row = iota((128, M), 0)

    def make_base(j, carry):
        slot = 10 * (4 * ((p_row >> 1) & 15) + (p_row >> 5)) + 2 * j + (p_row & 1)
        wave = jnp.sum(jnp.where(iota((128, M), 1) == slot, wave_row, 0.0), axis=1, keepdims=True)
        wave = jnp.broadcast_to(wave, (128, 128))
        c, s = unit(wave * iota((128, 128), 1).astype(F32), count, inverse)
        base[j, 0] = c
        base[j, 1] = s
        c, s = unit(wave * 128.0, count, inverse)
        base[j, 2] = c
        base[j, 3] = s
        return carry

    lax.fori_loop(0, PAIRS, make_base, 0)
    o_row, o_col = iota((256, 256), 0), iota((256, 256), 1)
    p256[...] = one_hot(o_col == (o_row & 15) * 16 + (o_row >> 4))
    pz[...] = one_hot(o_col == ((o_row >> 2) & 3) * 64 + ((o_row >> 1) & 1) * 32 + (o_row >> 4) * 2 + (o_row & 1))
    field_in.wait()
    fm[...] = jnp.where(iota((LEV, LONS), 1) < count_ref[0], fi[...].astype(F32), 0.0).astype(BF16)

    def transform(j):
        def rows(b, inner):
            at = pl.ds(pl.multiple_of(b * 32, 32), 32)
            c, s = base[j, 0, at, :], base[j, 1, at, :]
            cw, sw = base[j, 2, at, :], base[j, 3, at, :]
            for a in range(LONS // 128):
                tbl[0, at, a * 128:(a + 1) * 128] = c.astype(BF16)
                tbl[1, at, a * 128:(a + 1) * 128] = s.astype(BF16)
                c, s = c * cw - s * sw, c * sw + s * cw
            return inner

        lax.fori_loop(0, 4, rows, 0)
        summed = dot(tbl[...].reshape(256, LONS), fm[...], 1, 1) / count
        for xx in range(X):
            at = xx * 32
            xs[j, xx] = jnp.concatenate([summed[at:at + 32], summed[128 + at:160 + at]], axis=0).astype(BF16)

    def send_x(j):
        xg[j, x] = xs[j, x]

        def send(o, carry):
            other = (x + o) % X
            pltpu.make_async_remote_copy(
                src_ref=xs.at[j, other], dst_ref=xg.at[j, x], send_sem=xs_sem, recv_sem=xr_sem.at[j],
                device_id=(z * X + other, d), device_id_type=MESH).start()
            return carry

        lax.fori_loop(1, X, send, 0)

    def pass_on(j, target, place):
        pltpu.make_async_copy(xg.at[j, 0:X - 1], xg.at[j, 0:X - 1], xr_sem.at[j]).wait()
        moved = dot(pz[...], xg[j].reshape(256, LEV), 1, 0).astype(BF16)
        target[:, place:place + 16, :] = moved.reshape(Z, 16, LEV)

    def send_z(stage, source, target):
        target[z] = source[z]

        def send(o, carry):
            other, device = z_partner(o)
            pltpu.make_async_remote_copy(
                src_ref=source.at[other], dst_ref=target.at[z], send_sem=zs_sem.at[stage],
                recv_sem=zr_sem.at[stage], device_id=device, device_id_type=MESH).start()
            return carry

        lax.fori_loop(0, Z - 1, send, 0)

    transform(0)
    pl.semaphore_wait(barrier, Z - 1 + GROUP - 1)
    send_x(0)
    transform(1)
    send_x(1)
    pass_on(0, zs0, 0)
    send_z(0, zs0, zr0)
    transform(2)
    send_x(2)
    pass_on(1, zs1, 0)
    send_z(1, zs1, zr1)
    transform(3)
    send_x(3)
    pass_on(2, zs2, 0)
    send_z(2, zs2, zr2)
    transform(4)
    send_x(4)
    pass_on(3, zs3, 0)
    pass_on(4, zs3, 16)
    send_z(3, zs3, zr3)

    o_row, o_col = iota((128, 128), 0), iota((128, 128), 1)
    prow[...] = one_hot(o_col == ((o_row >> 4) & 1) * 64 + 4 * (o_row & 15) + (o_row >> 5))
    c_row = iota((256, 1), 0)
    i_main = total_wave(c_row >> 3, c_row & 7)
    i_left = total_wave(c_row >> 3, 8 + (c_row & 1))
    n_col = iota((256, M), 1)
    pcol[0:256] = one_hot(n_col == M - 1 - i_main)
    pcol[256:512] = one_hot(n_col == i_main)
    pcol[512:768] = one_hot(n_col == M - 1 - i_left)
    pcol[768:1024] = one_hot(n_col == i_left)

    lane_slot = (iota((1, 128), 1) >> 4) & 1
    left_j = (c_row >> 1) & 3

    def legendre(j):
        lr[j] = dot(prow[...], li[2 * j:2 * j + 2].reshape(128, M), 1, 0).astype(BF16)
        w0 = wave_ref[10 * lat + 2 * j]
        w1 = wave_ref[10 * lat + 2 * j + 1]
        low = jnp.minimum(w0, w1)
        small = jnp.where(lane_slot == 0, w0, w1) == low
        put = pcol[...]
        moved = dot(put, lr[j], 1, 1)
        upper, lower, upper_left, lower_left = (moved[a * 256:(a + 1) * 256] for a in range(4))
        high = jnp.where(small, upper, 0.0)
        deep = jnp.where(small, jnp.where(i_main >= low, lower, 0.0), jnp.where(i_main < low, upper, 0.0))
        if j >= 3:
            high, deep = high.reshape(GROUP, 8, 128), deep.reshape(GROUP, 8, 128)
            high, deep = (jnp.concatenate([high[:, a:a + 4], deep[:, a:a + 4]], axis=1).reshape(256, 128) for a in (0, 4))
        lu[j] = high.astype(BF16)
        lv[j] = deep.astype(BF16)
        here = left_j == j % 3
        lul[j] = jnp.where(here & small, upper_left, 0.0).astype(BF16)
        lvl[j] = jnp.where(small, jnp.where(here & (i_left >= low), lower_left, 0.0),
                           jnp.where(here & (i_left < low), upper_left, 0.0)).astype(BF16)
        pick = one_hot((iota((16, M), 0) == EXTRA[j]) & (iota((16, M), 1) == M - 1 - low))
        lw[j] = jnp.where(small, 0.0, dot(pick, lr[j], 1, 1)).astype(BF16)
        for xx in range(X):
            wave = wave_ref[10 * (X * z + xx) + 2 * j]
            mt[j, xx * 8:(xx + 1) * 8, :] = jnp.full((8, 128), jnp.minimum(wave, M - 1 - wave), jnp.int32)

    def rows_along_z(stage, source):
        pltpu.make_async_copy(source.at[0:Z - 1], source.at[0:Z - 1], zr_sem.at[stage]).wait()

    def gather(j, source, place):
        piece = source[:, place:place + 16, :].reshape(256, LEV)
        moved = dot(p256[...], piece, 1, 0).astype(BF16)
        for xx in range(X):
            for q in range(2):
                at = (xx * 4 + q * 2) * 16
                xr[j, xx, :, q * 128:(q + 1) * 128] = moved[at:at + 32]

    def both_kinds(up, low):
        return jnp.concatenate([up.reshape(GROUP, 8, 256), low.reshape(GROUP, 8, 256)], axis=1).astype(BF16)

    def spectral(j, target, place):
        rhs = xr[j].reshape(128, 256)
        target[:, place:place + 16, :] = both_kinds(dot(lu[j], rhs, 1, 0), dot(lv[j], rhs, 1, 0))

    def send_plane(stage, source, target):
        target[me] = source[me]

        for step in STEPS:
            other, device = plane_partner(step)
            pltpu.make_async_remote_copy(
                src_ref=source.at[other], dst_ref=target.at[me], send_sem=ps_sem.at[stage],
                recv_sem=pr_sem.at[stage], device_id=device, device_id_type=MESH).start()

    def left_over(js, target, place):
        up, low = jnp.zeros((256, 256), F32), jnp.zeros((256, 256), F32)
        extra = jnp.zeros((16, 256), F32)
        for j in js:
            rhs = xr[j].reshape(128, 256)
            up += dot(lul[j], rhs, 1, 0)
            low += dot(lvl[j], rhs, 1, 0)
            extra += dot(lw[j], rhs, 1, 0)
        up = up.reshape(GROUP, 8, 256) + extra[0:8][None]
        low = low.reshape(GROUP, 8, 256) + extra[8:16][None]
        target[:, place:place + 16, :] = both_kinds(up, low)

    leg_in.wait()
    legendre(0)
    rows_along_z(0, zr0)
    gather(0, zr0, 0)
    spectral(0, ps0, 0)
    send_plane(0, ps0, pr0)
    legendre(1)
    rows_along_z(1, zr1)
    gather(1, zr1, 0)
    spectral(1, ps1, 0)
    send_plane(1, ps1, pr1)
    legendre(2)
    rows_along_z(2, zr2)
    gather(2, zr2, 0)
    spectral(2, ps2, 0)
    left_over((0, 1, 2), ps2, 16)
    send_plane(2, ps2, pr2)
    legendre(3)
    legendre(4)

    def arrived(stage, target, subs):
        pltpu.make_async_copy(target.at[0:GROUP - 1], target.at[0:GROUP - 1], pr_sem.at[stage]).wait()
        for b, sub in enumerate(subs):
            for g in range(2):
                piece = target[g * 16:(g + 1) * 16, b * 16:(b + 1) * 16, :].reshape(256, 256)
                moved = dot(p256[...], piece, 1, 0).astype(BF16)
                ab[sub, :, g * 16:(g + 1) * 16, :] = moved.reshape(16, 16, 256)

    def halves(rows):
        return jnp.concatenate([rows[:, 0:128], rows[:, 128:256]], axis=0)

    def waves_of(js):
        tile = jnp.concatenate([mt[j] for j in js], axis=0)
        return jnp.concatenate([tile, tile], axis=0)

    def gram(k, ups, lows, js, first, extras=None, extra_js=()):
        i = total_wave(me, k)
        up = halves(jnp.concatenate(ups, axis=0))
        low = halves(jnp.concatenate(lows, axis=0))
        waves = waves_of(js)
        inside = low * one_hot(waves <= i)
        outside = low * one_hot(waves > i)
        near = dot(low, inside, 0, 0)
        far = dot(up, up, 0, 0) + dot(low, outside, 0, 0)
        if extras is not None:
            far += dot(extras, extras * one_hot(waves_of(extra_js) == i), 0, 0)
        if first:
            acc[k, 0] = near
            acc[k, 1] = far
        else:
            acc[k, 0] += near
            acc[k, 1] += far

    arrived(0, pr0, (0,))

    def gram_a(k, carry):
        gram(k, [ab[0, k]], [ab[0, 8 + k]], (0,), True)
        return carry

    lax.fori_loop(0, 8, gram_a, 0)

    rows_along_z(3, zr3)
    gather(3, zr3, 0)
    gather(4, zr3, 16)
    left_over((3, 4), ps3, 0)
    send_plane(3, ps3, pr3)
    rhs3, rhs4 = xr[3].reshape(128, 256), xr[4].reshape(128, 256)
    ps4[...] = both_kinds(dot(lu[3], rhs3, 1, 0), dot(lu[4], rhs4, 1, 0))
    send_plane(4, ps4, pr4)
    ps5[...] = both_kinds(dot(lv[3], rhs3, 1, 0), dot(lv[4], rhs4, 1, 0))
    send_plane(5, ps5, pr5)

    arrived(1, pr1, (1,))
    arrived(2, pr2, (2, 5))
    extras_b = halves(jnp.concatenate([ab[5, EXTRA[j]] for j in (0, 1, 2)], axis=0))

    def gram_b(k, carry):
        gram(k, [ab[1, k], ab[2, k]], [ab[1, 8 + k], ab[2, 8 + k]], (1, 2), False, extras_b, (0, 1, 2))
        return carry

    lax.fori_loop(0, 8, gram_b, 0)
    for kk in range(2):
        gram(8 + kk, [ab[5, 2 * j + kk] for j in range(3)], [ab[5, 8 + 2 * j + kk] for j in range(3)],
             (0, 1, 2), True, extras_b, (0, 1, 2))

    lane = iota((16, 128), 1)

    behind = 1 + d % 2

    def owner_of(k):
        return (d + 8 * k) // 5

    def toward(k):
        return (owner_of(k) - z + Z + behind) % 4 - behind

    def pack_send(k):
        for h in range(2):
            whole = acc[k, h]
            blocks = [whole[0:16]]
            for r in range(1, 4):
                folded = pltpu.roll(whole[16 * (8 - r):16 * (9 - r)], 16 * r, 1)
                blocks.append(jnp.where(lane >= 16 * r, whole[16 * r:16 * (r + 1)], folded))
            blocks.append(whole[64:80])
            rs[k, h * 80:(h + 1) * 80, :] = jnp.concatenate(blocks, axis=0).astype(BF16)
        step = toward(k)
        seat = step + behind

        @pl.when(step != 0)
        def _():
            pltpu.make_async_remote_copy(
                src_ref=rs.at[k], dst_ref=r1.at[k, seat - (seat + 3 - behind) // 4], send_sem=r1s_sem,
                recv_sem=r1_sem.at[k], device_id=(((z + step + Z) % Z) * X + x, d), device_id_type=MESH).start()

    keep = (iota((128, 128), 1) >> 4) >= (iota((128, 128), 0) >> 4)

    def level_two(k, carry):
        @pl.when(toward(k) == 0)
        def _():
            pltpu.make_async_copy(r1.at[k], r1.at[k], r1_sem.at[k]).wait()
            total = rs[k].astype(F32)
            for a in range(3):
                total += r1[k, a].astype(F32)
            for h in range(2):
                part = total[h * 80:(h + 1) * 80]
                blocks = [part[16 * r:16 * (r + 1)] for r in range(5)]
                for r in range(3, 0, -1):
                    blocks.append(pltpu.roll(part[16 * r:16 * (r + 1)], 128 - 16 * r, 1))
                upper = jnp.concatenate(blocks, axis=0)
                r2s[k, :, h] = jnp.where(keep, upper, upper.T).astype(BF16).reshape(D, 16, 128)
            owner = owner_of(k)
            seat = (d + 8 * k) % 5 * 4 + z // 4

            def send(o, inner):
                other = (d + o) % D
                pltpu.make_async_remote_copy(
                    src_ref=r2s.at[k, other], dst_ref=r2.at[seat], send_sem=r2s_sem, recv_sem=r2_sem,
                    device_id=(owner * X + x, other), device_id_type=MESH).start()
                return inner

            lax.fori_loop(1, D, send, 0)

            @pl.when(owner == z)
            def _():
                r2[seat] = r2s[k, d]

            @pl.when(owner != z)
            def _():
                send(0, 0)

        return carry

    arrived(3, pr3, (6,))
    extras_c = halves(jnp.concatenate([ab[6, EXTRA[j]] for j in (3, 4)], axis=0))

    def gram_left(kk, carry):
        gram(8 + kk, [ab[6, kk], ab[6, 2 + kk]], [ab[6, 8 + kk], ab[6, 10 + kk]], (3, 4), False, extras_c, (3, 4))
        pack_send(8 + kk)
        return carry

    lax.fori_loop(0, 2, gram_left, 0)
    for half, (source, sub) in enumerate(((pr4, 3), (pr5, 4))):
        arrived(4 + half, source, (sub,))

        def gram_c(k, carry, sub=sub, half=half):
            gram(4 * half + k, [ab[sub, k], ab[sub, 8 + k]], [ab[sub, 4 + k], ab[sub, 12 + k]], (3, 4), False,
                 extras_c, (3, 4))
            pack_send(4 * half + k)
            return carry

        lax.fori_loop(0, 4, gram_c, 0)
        if half == 0:
            lax.fori_loop(8, OWN, level_two, 0)

    lax.fori_loop(0, 4, level_two, 0)
    lax.fori_loop(4, 8, level_two, 0)
    holds = (d + 3 * z) % 8 < 5

    @pl.when(holds)
    def _():
        pltpu.make_async_copy(r2.at[0:19], r2.at[0:19], r2_sem).wait()

    @pl.when(jnp.logical_not(holds))
    def _():
        pltpu.make_async_copy(r2, r2, r2_sem).wait()

    for u in range(5):
        total = r2[4 * u].astype(F32)
        for a in range(1, 4):
            total += r2[4 * u + a].astype(F32)
        out_ref[:, u] = total * 0.125

    for stage, source in enumerate((zs0, zs1, zs2, zs3)):
        pltpu.make_async_copy(source.at[0:Z - 1], source.at[0:Z - 1], zs_sem.at[stage]).wait()
    for j in range(PAIRS):
        pltpu.make_async_copy(xs.at[j, 0:X - 1], xs.at[j, 0:X - 1], xs_sem).wait()
    for stage, source in enumerate((ps0, ps1, ps2, ps3, ps4, ps5)):
        pltpu.make_async_copy(source.at[0:GROUP - 1], source.at[0:GROUP - 1], ps_sem.at[stage]).wait()

    def sent(k, carry):
        @pl.when(toward(k) != 0)
        def _():
            pltpu.make_async_copy(rs.at[k], rs.at[k], r1s_sem).wait()

        @pl.when((toward(k) == 0) & (owner_of(k) != z))
        def _():
            pltpu.make_async_copy(r2s.at[k], r2s.at[k], r2s_sem).wait()

        @pl.when(owner_of(k) == z)
        def _():
            pltpu.make_async_copy(r2s.at[k, 0:D - 1], r2s.at[k, 0:D - 1], r2s_sem).wait()

        return carry

    lax.fori_loop(0, OWN, sent, 0)


def per_device(field, lon_count, wave_order, legendre):
    vmem = pl.BlockSpec(memory_space=pltpu.VMEM)
    smem = pl.BlockSpec(memory_space=pltpu.SMEM)
    V = pltpu.VMEM
    scratch = [
        V((LEV, LONS), BF16), V((2 * PAIRS, NLAT, M), BF16),
        V((LEV, LONS), BF16), V((2, 128, LONS), BF16), V((PAIRS, 4, 128, 128), F32),
        V((PAIRS, X, 64, LEV), BF16), V((PAIRS, X, 64, LEV), BF16),
        *[V((Z, rows, LEV), BF16) for rows in (16, 16, 16, 32)] * 2, V((PAIRS, X, 32, 256), BF16), V((256, 256), BF16),
        V((256, 256), BF16), V((128, 128), BF16), V((1024, M), BF16), V((PAIRS, 128, M), BF16),
        V((PAIRS, 256, 128), BF16), V((PAIRS, 256, 128), BF16),
        V((PAIRS, 256, 128), BF16), V((PAIRS, 256, 128), BF16), V((PAIRS, 16, 128), BF16),
        *[V((GROUP, rows, 256), BF16) for rows in (16, 16, 32, 16, 16, 16)] * 2,
        V((7, 16, GROUP, 256), BF16), V((PAIRS, 32, 128), jnp.int32), V((OWN, 2, 128, 128), F32),
        V((OWN, 160, 128), BF16), V((OWN, 3, 160, 128), BF16), V((OWN, D, 2, 16, 128), BF16),
        V((20, 2, 16, 128), BF16),
        pltpu.SemaphoreType.DMA((2,)),
        pltpu.SemaphoreType.DMA((4,)), pltpu.SemaphoreType.DMA((4,)),
        pltpu.SemaphoreType.DMA, pltpu.SemaphoreType.DMA((PAIRS,)),
        pltpu.SemaphoreType.DMA((6,)), pltpu.SemaphoreType.DMA((6,)),
        pltpu.SemaphoreType.DMA, pltpu.SemaphoreType.DMA((OWN,)),
        pltpu.SemaphoreType.DMA, pltpu.SemaphoreType.DMA,
    ]
    hbm = pl.BlockSpec(memory_space=pltpu.HBM)
    return pl.pallas_call(
        kernel,
        out_shape=jax.ShapeDtypeStruct((2, 5, 16, 128), F32),
        in_specs=[smem, smem, vmem, hbm, hbm],
        out_specs=vmem,
        scratch_shapes=scratch,
        compiler_params=pltpu.CompilerParams(
            collective_id=0, has_side_effects=True, vmem_limit_bytes=60 * 1024 * 1024),
    )(lon_count, wave_order, wave_order, field.reshape(LEV, LONS), legendre)


def solution(mesh):
    return jax.shard_map(
        per_device,
        mesh=mesh,
        in_specs=(P("mem", "lat", None, None), P("lat"), P(), P("lat", None, None)),
        out_specs=P(None, "lat", "mem", None),
        check_vma=False,
    )
```

```python
import jax
import jax.numpy as jnp
from jax import lax
from jax.experimental import pallas as pl
from jax.experimental.pallas import tpu as pltpu
from jax.sharding import PartitionSpec as P

MESH = pl.DeviceIdType.MESH
F32 = jnp.float32
BF16 = jnp.bfloat16
Z, X, D = 16, 4, 8
GROUP = X * D
LEV, LONS, M, NLAT = 128, 2688, 640, 64
PAIRS = 5
EXTRA = (6, 7, 14, 4, 5)
OWN = 10
COS = (1.0, -19.739208221435547, 64.93939208984375, -85.45681762695312, 60.24457931518555,
       -26.425565719604492, 7.898900985717773, -1.6961979866027832, 0.24304766952991486)
SIN = (6.2831854820251465, -41.34170150756836, 81.6052474975586, -76.70585632324219, 42.05867385864258,
       -15.094411849975586, 3.818404197692871, -0.7120527029037476, 0.09126123040914536)


STEPS = sorted(((dx, dy, dc) for dx in range(4) for dy in range(4) for dc in range(2) if dx or dy or dc),
               key=lambda s: -min(s[0], 4 - s[0]) - min(s[1], 4 - s[1]))


def iota(shape, dim):
    return lax.broadcasted_iota(jnp.int32, shape, dim)


def dot(a, b, ca, cb):
    return lax.dot_general(a, b, (((ca,), (cb,)), ((), ())), preferred_element_type=F32)


def poly(coefficients, v):
    total = jnp.full_like(v, coefficients[-1])
    for value in coefficients[-2::-1]:
        total = total * v + value
    return total


def unit(product, count, inverse):
    turns = jnp.floor(product * inverse + 0.5)
    u = (product - turns * count) * inverse
    v = u * u
    return poly(COS, v), -u * poly(SIN, v)


def one_hot(condition):
    return jnp.where(condition, 1.0, 0.0).astype(BF16)


def total_wave(dest, k):
    t = (dest & 7) + 8 * k
    zz = (t * 205) >> 10
    return 20 * zz + 5 * (dest >> 3) + (t - 5 * zz)


def kernel(count_ref, wave_ref, waves_ref, field_ref, leg_ref, out_ref,
           fi, li, fm, tbl, base, xs, xg, zs0, zs1, zs2, zs3, zr0, zr1, zr2, zr3, xr, p256, pz, prow, pcol, lr, lu, lv, lul, lvl, lw,
           ps0, ps1, ps2, ps3, ps4, ps5, pr0, pr1, pr2, pr3, pr4, pr5, ab, mt, acc, rs, r1, r2s, r2,
           in_sem, zs_sem, zr_sem, xs_sem, xr_sem, ps_sem, pr_sem, r1s_sem, r1_sem, r2s_sem, r2_sem):
    field_in = pltpu.make_async_copy(field_ref, fi, in_sem.at[0])
    leg_in = pltpu.make_async_copy(leg_ref, li, in_sem.at[1])
    field_in.start()
    leg_in.start()
    lat = lax.axis_index("lat")
    d = lax.axis_index("mem")
    z, x = lat // X, lat % X
    me = x * D + d

    def z_partner(o):
        far = 8 - (o + 1) // 2
        other = (z + far + (1 - o % 2) * (Z - 2 * far)) % Z
        return other, (other * X + x, d)

    def plane_partner(step):
        other_x = (x + step[0]) % X
        other_d = (d // 2 + step[1]) % 4 * 2 + (d + step[2]) % 2
        return other_x * D + other_d, (z * X + other_x, other_d)

    barrier = pltpu.get_barrier_semaphore()

    for o in range(Z - 1):
        pl.semaphore_signal(barrier, inc=1, device_id=z_partner(o)[1], device_id_type=MESH)
    for o in range(1, X):
        pl.semaphore_signal(barrier, inc=1, device_id=(z * X + (x + o) % X, d), device_id_type=MESH)
    for o in range(1, D):
        pl.semaphore_signal(barrier, inc=1, device_id=(lat, (d + o) % D), device_id_type=MESH)

    count = count_ref[0].astype(F32)
    inverse = 1.0 / jnp.full((128, 128), count, F32)
    wave_row = waves_ref[...].astype(F32).reshape(1, M)
    p_row = iota((128, M), 0)

    def make_base(j, carry):
        slot = 10 * (4 * ((p_row >> 1) & 15) + (p_row >> 5)) + 2 * j + (p_row & 1)
        wave = jnp.sum(jnp.where(iota((128, M), 1) == slot, wave_row, 0.0), axis=1, keepdims=True)
        wave = jnp.broadcast_to(wave, (128, 128))
        c, s = unit(wave * iota((128, 128), 1).astype(F32), count, inverse)
        base[j, 0] = c
        base[j, 1] = s
        c, s = unit(wave * 128.0, count, inverse)
        base[j, 2] = c
        base[j, 3] = s
        return carry

    make_base(0, 0)
    field_in.wait()
    fm[...] = jnp.where(iota((LEV, LONS), 1) < count_ref[0], fi[...].astype(F32), 0.0).astype(BF16)

    def transform(j):
        def rows(b, inner):
            at = pl.ds(pl.multiple_of(b * 32, 32), 32)
            c, s = base[j, 0, at, :], base[j, 1, at, :]
            cw, sw = base[j, 2, at, :], base[j, 3, at, :]
            for a in range(LONS // 128):
                tbl[0, at, a * 128:(a + 1) * 128] = c.astype(BF16)
                tbl[1, at, a * 128:(a + 1) * 128] = s.astype(BF16)
                c, s = c * cw - s * sw, c * sw + s * cw
            return inner

        lax.fori_loop(0, 4, rows, 0)
        summed = dot(tbl[...].reshape(256, LONS), fm[...], 1, 1) / count
        for xx in range(X):
            at = xx * 32
            xs[j, xx] = jnp.concatenate([summed[at:at + 32], summed[128 + at:160 + at]], axis=0).astype(BF16)

    def send_x(j):
        xg[j, x] = xs[j, x]

        for o in range(1, X):
            other = (x + o) % X
            pltpu.make_async_remote_copy(
                src_ref=xs.at[j, other], dst_ref=xg.at[j, x], send_sem=xs_sem, recv_sem=xr_sem.at[j],
                device_id=(z * X + other, d), device_id_type=MESH).start()

    def pass_on(j, target, place):
        pltpu.make_async_copy(xg.at[j, 0:X - 1], xg.at[j, 0:X - 1], xr_sem.at[j]).wait()
        moved = dot(pz[...], xg[j].reshape(256, LEV), 1, 0).astype(BF16)
        target[:, place:place + 16, :] = moved.reshape(Z, 16, LEV)

    def send_z(stage, source, target):
        target[z] = source[z]

        for o in range(Z - 1):
            other, device = z_partner(o)
            pltpu.make_async_remote_copy(
                src_ref=source.at[other], dst_ref=target.at[z], send_sem=zs_sem.at[stage],
                recv_sem=zr_sem.at[stage], device_id=device, device_id_type=MESH).start()

    transform(0)
    pl.semaphore_wait(barrier, Z - 1 + X - 1 + D - 1)
    send_x(0)
    lax.fori_loop(1, PAIRS, make_base, 0)
    o_row, o_col = iota((256, 256), 0), iota((256, 256), 1)
    p256[...] = one_hot(o_col == (o_row & 15) * 16 + (o_row >> 4))
    pz[...] = one_hot(o_col == ((o_row >> 2) & 3) * 64 + ((o_row >> 1) & 1) * 32 + (o_row >> 4) * 2 + (o_row & 1))
    transform(1)
    send_x(1)
    pass_on(0, zs0, 0)
    send_z(0, zs0, zr0)
    transform(2)
    send_x(2)
    pass_on(1, zs1, 0)
    send_z(1, zs1, zr1)
    transform(3)
    send_x(3)
    transform(4)
    send_x(4)
    pass_on(2, zs2, 0)
    send_z(2, zs2, zr2)
    pass_on(3, zs3, 0)
    pass_on(4, zs3, 16)
    send_z(3, zs3, zr3)

    o_row, o_col = iota((128, 128), 0), iota((128, 128), 1)
    prow[...] = one_hot(o_col == ((o_row >> 4) & 1) * 64 + 4 * (o_row & 15) + (o_row >> 5))
    c_row = iota((256, 1), 0)
    i_main = total_wave(c_row >> 3, c_row & 7)
    i_left = total_wave(c_row >> 3, 8 + (c_row & 1))
    n_col = iota((256, M), 1)
    pcol[0:256] = one_hot(n_col == M - 1 - i_main)
    pcol[256:512] = one_hot(n_col == i_main)
    pcol[512:768] = one_hot(n_col == M - 1 - i_left)
    pcol[768:1024] = one_hot(n_col == i_left)

    lane_slot = (iota((1, 128), 1) >> 4) & 1
    left_j = (c_row >> 1) & 3

    def legendre(j):
        lr[j] = dot(prow[...], li[2 * j:2 * j + 2].reshape(128, M), 1, 0).astype(BF16)
        w0 = wave_ref[10 * lat + 2 * j]
        w1 = wave_ref[10 * lat + 2 * j + 1]
        low = jnp.minimum(w0, w1)
        small = jnp.where(lane_slot == 0, w0, w1) == low
        put = pcol[...]
        moved = dot(put, lr[j], 1, 1)
        upper, lower, upper_left, lower_left = (moved[a * 256:(a + 1) * 256] for a in range(4))
        high = jnp.where(small, upper, 0.0)
        deep = jnp.where(small, jnp.where(i_main >= low, lower, 0.0), jnp.where(i_main < low, upper, 0.0))
        if j >= 3:
            high, deep = high.reshape(GROUP, 8, 128), deep.reshape(GROUP, 8, 128)
            high, deep = (jnp.concatenate([high[:, a:a + 4], deep[:, a:a + 4]], axis=1).reshape(256, 128) for a in (0, 4))
        lu[j] = high.astype(BF16)
        lv[j] = deep.astype(BF16)
        here = left_j == j % 3
        lul[j] = jnp.where(here & small, upper_left, 0.0).astype(BF16)
        lvl[j] = jnp.where(small, jnp.where(here & (i_left >= low), lower_left, 0.0),
                           jnp.where(here & (i_left < low), upper_left, 0.0)).astype(BF16)
        pick = one_hot((iota((16, M), 0) == EXTRA[j]) & (iota((16, M), 1) == M - 1 - low))
        lw[j] = jnp.where(small, 0.0, dot(pick, lr[j], 1, 1)).astype(BF16)
        for xx in range(X):
            wave = wave_ref[10 * (X * z + xx) + 2 * j]
            mt[j, xx * 8:(xx + 1) * 8, :] = jnp.full((8, 128), jnp.minimum(wave, M - 1 - wave), jnp.int32)

    def rows_along_z(stage, source):
        pltpu.make_async_copy(source.at[0:Z - 1], source.at[0:Z - 1], zr_sem.at[stage]).wait()

    def gather(j, source, place):
        piece = source[:, place:place + 16, :].reshape(256, LEV)
        moved = dot(p256[...], piece, 1, 0).astype(BF16)
        for xx in range(X):
            for q in range(2):
                at = (xx * 4 + q * 2) * 16
                xr[j, xx, :, q * 128:(q + 1) * 128] = moved[at:at + 32]

    def both_kinds(up, low):
        return jnp.concatenate([up.reshape(GROUP, 8, 256), low.reshape(GROUP, 8, 256)], axis=1).astype(BF16)

    def spectral(j, target, place):
        rhs = xr[j].reshape(128, 256)
        target[:, place:place + 16, :] = both_kinds(dot(lu[j], rhs, 1, 0), dot(lv[j], rhs, 1, 0))

    def send_plane(stage, source, target):
        target[me] = source[me]

        for step in STEPS:
            other, device = plane_partner(step)
            pltpu.make_async_remote_copy(
                src_ref=source.at[other], dst_ref=target.at[me], send_sem=ps_sem.at[stage],
                recv_sem=pr_sem.at[stage], device_id=device, device_id_type=MESH).start()

    def left_over(js, target, place):
        up, low = jnp.zeros((256, 256), F32), jnp.zeros((256, 256), F32)
        extra = jnp.zeros((16, 256), F32)
        for j in js:
            rhs = xr[j].reshape(128, 256)
            up += dot(lul[j], rhs, 1, 0)
            low += dot(lvl[j], rhs, 1, 0)
            extra += dot(lw[j], rhs, 1, 0)
        up = up.reshape(GROUP, 8, 256) + extra[0:8][None]
        low = low.reshape(GROUP, 8, 256) + extra[8:16][None]
        target[:, place:place + 16, :] = both_kinds(up, low)

    leg_in.wait()
    legendre(0)
    rows_along_z(0, zr0)
    gather(0, zr0, 0)
    spectral(0, ps0, 0)
    send_plane(0, ps0, pr0)
    legendre(1)
    rows_along_z(1, zr1)
    gather(1, zr1, 0)
    spectral(1, ps1, 0)
    send_plane(1, ps1, pr1)
    legendre(2)
    rows_along_z(2, zr2)
    gather(2, zr2, 0)
    spectral(2, ps2, 0)
    left_over((0, 1, 2), ps2, 16)
    send_plane(2, ps2, pr2)
    legendre(3)
    legendre(4)

    def arrived(stage, target, subs, then=None):
        pltpu.make_async_copy(target.at[0:GROUP - 1], target.at[0:GROUP - 1], pr_sem.at[stage]).wait()
        if then is not None:
            send_plane(*then)
        for b, sub in enumerate(subs):
            for g in range(2):
                piece = target[g * 16:(g + 1) * 16, b * 16:(b + 1) * 16, :].reshape(256, 256)
                moved = dot(p256[...], piece, 1, 0).astype(BF16)
                ab[sub, :, g * 16:(g + 1) * 16, :] = moved.reshape(16, 16, 256)

    def halves(rows):
        return jnp.concatenate([rows[:, 0:128], rows[:, 128:256]], axis=0)

    def waves_of(js):
        tile = jnp.concatenate([mt[j] for j in js], axis=0)
        return jnp.concatenate([tile, tile], axis=0)

    def gram(k, ups, lows, js, first, extras=None, extra_js=()):
        i = total_wave(me, k)
        up = halves(jnp.concatenate(ups, axis=0))
        low = halves(jnp.concatenate(lows, axis=0))
        waves = waves_of(js)
        inside = low * one_hot(waves <= i)
        outside = low * one_hot(waves > i)
        near = dot(low, inside, 0, 0)
        far = dot(up, up, 0, 0) + dot(low, outside, 0, 0)
        if extras is not None:
            far += dot(extras, extras * one_hot(waves_of(extra_js) == i), 0, 0)
        if first:
            acc[k, 0] = near
            acc[k, 1] = far
        else:
            acc[k, 0] += near
            acc[k, 1] += far

    arrived(0, pr0, (0,))

    def gram_a(k, carry):
        gram(k, [ab[0, k]], [ab[0, 8 + k]], (0,), True)
        return carry

    lax.fori_loop(0, 8, gram_a, 0)

    rows_along_z(3, zr3)
    gather(3, zr3, 0)
    gather(4, zr3, 16)
    left_over((3, 4), ps3, 0)
    send_plane(3, ps3, pr3)
    rhs3, rhs4 = xr[3].reshape(128, 256), xr[4].reshape(128, 256)
    ps4[...] = both_kinds(dot(lu[3], rhs3, 1, 0), dot(lu[4], rhs4, 1, 0))
    ps5[...] = both_kinds(dot(lv[3], rhs3, 1, 0), dot(lv[4], rhs4, 1, 0))

    arrived(1, pr1, (1,))
    arrived(2, pr2, (2, 5), (4, ps4, pr4))
    extras_b = halves(jnp.concatenate([ab[5, EXTRA[j]] for j in (0, 1, 2)], axis=0))

    def gram_b(k, carry):
        gram(k, [ab[1, k], ab[2, k]], [ab[1, 8 + k], ab[2, 8 + k]], (1, 2), False, extras_b, (0, 1, 2))
        return carry

    lax.fori_loop(0, 8, gram_b, 0)
    for kk in range(2):
        gram(8 + kk, [ab[5, 2 * j + kk] for j in range(3)], [ab[5, 8 + 2 * j + kk] for j in range(3)],
             (0, 1, 2), True, extras_b, (0, 1, 2))

    lane = iota((16, 128), 1)

    behind = 1 + d % 2

    def owner_of(k):
        return (d + 8 * k) // 5

    def toward(k):
        return (owner_of(k) - z + Z + behind) % 4 - behind

    def pack_send(k):
        for h in range(2):
            whole = acc[k, h]
            blocks = [whole[0:16]]
            for r in range(1, 4):
                folded = pltpu.roll(whole[16 * (8 - r):16 * (9 - r)], 16 * r, 1)
                blocks.append(jnp.where(lane >= 16 * r, whole[16 * r:16 * (r + 1)], folded))
            blocks.append(whole[64:80])
            rs[k, h * 80:(h + 1) * 80, :] = jnp.concatenate(blocks, axis=0).astype(BF16)
        step = toward(k)
        seat = step + behind

        @pl.when(step != 0)
        def _():
            pltpu.make_async_remote_copy(
                src_ref=rs.at[k], dst_ref=r1.at[k, seat - (seat + 3 - behind) // 4], send_sem=r1s_sem,
                recv_sem=r1_sem.at[k], device_id=(((z + step + Z) % Z) * X + x, d), device_id_type=MESH).start()

    keep = (iota((128, 128), 1) >> 4) >= (iota((128, 128), 0) >> 4)

    def level_two(k, carry):
        @pl.when(toward(k) == 0)
        def _():
            pltpu.make_async_copy(r1.at[k], r1.at[k], r1_sem.at[k]).wait()
            total = rs[k].astype(F32)
            for a in range(3):
                total += r1[k, a].astype(F32)
            for h in range(2):
                part = total[h * 80:(h + 1) * 80]
                blocks = [part[16 * r:16 * (r + 1)] for r in range(5)]
                for r in range(3, 0, -1):
                    blocks.append(pltpu.roll(part[16 * r:16 * (r + 1)], 128 - 16 * r, 1))
                upper = jnp.concatenate(blocks, axis=0)
                r2s[k, :, h] = jnp.where(keep, upper, upper.T).astype(BF16).reshape(D, 16, 128)
            owner = owner_of(k)
            seat = (d + 8 * k) % 5 * 4 + z // 4

            def send(o):
                other = (d + o) % D
                pltpu.make_async_remote_copy(
                    src_ref=r2s.at[k, other], dst_ref=r2.at[seat], send_sem=r2s_sem, recv_sem=r2_sem,
                    device_id=(owner * X + x, other), device_id_type=MESH).start()

            for o in range(1, D):
                send(o)

            @pl.when(owner == z)
            def _():
                r2[seat] = r2s[k, d]

            @pl.when(owner != z)
            def _():
                send(0)

        return carry

    arrived(3, pr3, (6,), (5, ps5, pr5))
    extras_c = halves(jnp.concatenate([ab[6, EXTRA[j]] for j in (3, 4)], axis=0))

    def gram_left(kk, carry):
        gram(8 + kk, [ab[6, kk], ab[6, 2 + kk]], [ab[6, 8 + kk], ab[6, 10 + kk]], (3, 4), False, extras_c, (3, 4))
        pack_send(8 + kk)
        return carry

    lax.fori_loop(0, 2, gram_left, 0)
    for half, (source, sub) in enumerate(((pr4, 3), (pr5, 4))):
        arrived(4 + half, source, (sub,))

        def gram_c(k, carry, sub=sub, half=half):
            gram(4 * half + k, [ab[sub, k], ab[sub, 8 + k]], [ab[sub, 4 + k], ab[sub, 12 + k]], (3, 4), False,
                 extras_c, (3, 4))
            pack_send(4 * half + k)
            return carry

        lax.fori_loop(0, 4, gram_c, 0)
        if half == 0:
            lax.fori_loop(8, OWN, level_two, 0)

    lax.fori_loop(0, 4, level_two, 0)
    lax.fori_loop(4, 8, level_two, 0)
    holds = (d + 3 * z) % 8 < 5

    @pl.when(holds)
    def _():
        pltpu.make_async_copy(r2.at[0:19], r2.at[0:19], r2_sem).wait()

    @pl.when(jnp.logical_not(holds))
    def _():
        pltpu.make_async_copy(r2, r2, r2_sem).wait()

    for u in range(5):
        total = r2[4 * u].astype(F32)
        for a in range(1, 4):
            total += r2[4 * u + a].astype(F32)
        out_ref[:, u] = total * 0.125

    for stage, source in enumerate((zs0, zs1, zs2, zs3)):
        pltpu.make_async_copy(source.at[0:Z - 1], source.at[0:Z - 1], zs_sem.at[stage]).wait()
    for j in range(PAIRS):
        pltpu.make_async_copy(xs.at[j, 0:X - 1], xs.at[j, 0:X - 1], xs_sem).wait()
    for stage, source in enumerate((ps0, ps1, ps2, ps3, ps4, ps5)):
        pltpu.make_async_copy(source.at[0:GROUP - 1], source.at[0:GROUP - 1], ps_sem.at[stage]).wait()

    def sent(k, carry):
        @pl.when(toward(k) != 0)
        def _():
            pltpu.make_async_copy(rs.at[k], rs.at[k], r1s_sem).wait()

        @pl.when((toward(k) == 0) & (owner_of(k) != z))
        def _():
            pltpu.make_async_copy(r2s.at[k], r2s.at[k], r2s_sem).wait()

        @pl.when(owner_of(k) == z)
        def _():
            pltpu.make_async_copy(r2s.at[k, 0:D - 1], r2s.at[k, 0:D - 1], r2s_sem).wait()

        return carry

    lax.fori_loop(0, OWN, sent, 0)


def per_device(field, lon_count, wave_order, legendre):
    vmem = pl.BlockSpec(memory_space=pltpu.VMEM)
    smem = pl.BlockSpec(memory_space=pltpu.SMEM)
    V = pltpu.VMEM
    scratch = [
        V((LEV, LONS), BF16), V((2 * PAIRS, NLAT, M), BF16),
        V((LEV, LONS), BF16), V((2, 128, LONS), BF16), V((PAIRS, 4, 128, 128), F32),
        V((PAIRS, X, 64, LEV), BF16), V((PAIRS, X, 64, LEV), BF16),
        *[V((Z, rows, LEV), BF16) for rows in (16, 16, 16, 32)] * 2, V((PAIRS, X, 32, 256), BF16), V((256, 256), BF16),
        V((256, 256), BF16), V((128, 128), BF16), V((1024, M), BF16), V((PAIRS, 128, M), BF16),
        V((PAIRS, 256, 128), BF16), V((PAIRS, 256, 128), BF16),
        V((PAIRS, 256, 128), BF16), V((PAIRS, 256, 128), BF16), V((PAIRS, 16, 128), BF16),
        *[V((GROUP, rows, 256), BF16) for rows in (16, 16, 32, 16, 16, 16)] * 2,
        V((7, 16, GROUP, 256), BF16), V((PAIRS, 32, 128), jnp.int32), V((OWN, 2, 128, 128), F32),
        V((OWN, 160, 128), BF16), V((OWN, 3, 160, 128), BF16), V((OWN, D, 2, 16, 128), BF16),
        V((20, 2, 16, 128), BF16),
        pltpu.SemaphoreType.DMA((2,)),
        pltpu.SemaphoreType.DMA((4,)), pltpu.SemaphoreType.DMA((4,)),
        pltpu.SemaphoreType.DMA, pltpu.SemaphoreType.DMA((PAIRS,)),
        pltpu.SemaphoreType.DMA((6,)), pltpu.SemaphoreType.DMA((6,)),
        pltpu.SemaphoreType.DMA, pltpu.SemaphoreType.DMA((OWN,)),
        pltpu.SemaphoreType.DMA, pltpu.SemaphoreType.DMA,
    ]
    hbm = pl.BlockSpec(memory_space=pltpu.HBM)
    return pl.pallas_call(
        kernel,
        out_shape=jax.ShapeDtypeStruct((2, 5, 16, 128), F32),
        in_specs=[smem, smem, vmem, hbm, hbm],
        out_specs=vmem,
        scratch_shapes=scratch,
        compiler_params=pltpu.CompilerParams(
            collective_id=0, has_side_effects=True, vmem_limit_bytes=60 * 1024 * 1024),
    )(lon_count, wave_order, wave_order, field.reshape(LEV, LONS), legendre)


def solution(mesh):
    return jax.shard_map(
        per_device,
        mesh=mesh,
        in_specs=(P("mem", "lat", None, None), P("lat"), P(), P("lat", None, None)),
        out_specs=P(None, "lat", "mem", None),
        check_vma=False,
    )
```

```python
import jax
import jax.numpy as jnp
from jax import lax
from jax.experimental import pallas as pl
from jax.experimental.pallas import tpu as pltpu
from jax.sharding import PartitionSpec as P

MESH = pl.DeviceIdType.MESH
F32 = jnp.float32
BF16 = jnp.bfloat16
Z, X, D = 16, 4, 8
GROUP = X * D
LEV, LONS, M, NLAT = 128, 2688, 640, 64
PAIRS = 5
EXTRA = (6, 7, 14, 4, 5)
OWN = 10
COS = (1.0, -19.739208221435547, 64.93939208984375, -85.45681762695312, 60.24457931518555,
       -26.425565719604492, 7.898900985717773, -1.6961979866027832, 0.24304766952991486)
SIN = (6.2831854820251465, -41.34170150756836, 81.6052474975586, -76.70585632324219, 42.05867385864258,
       -15.094411849975586, 3.818404197692871, -0.7120527029037476, 0.09126123040914536)


STEPS = sorted(((dx, dy, dc) for dx in range(4) for dy in range(4) for dc in range(2) if dx or dy or dc),
               key=lambda s: (11 * (s[0] * 8 + s[1] * 2 + s[2])) % 32)


def iota(shape, dim):
    return lax.broadcasted_iota(jnp.int32, shape, dim)


def dot(a, b, ca, cb):
    return lax.dot_general(a, b, (((ca,), (cb,)), ((), ())), preferred_element_type=F32)


def poly(coefficients, v):
    total = jnp.full_like(v, coefficients[-1])
    for value in coefficients[-2::-1]:
        total = total * v + value
    return total


def unit(product, count, inverse):
    turns = jnp.floor(product * inverse + 0.5)
    u = (product - turns * count) * inverse
    v = u * u
    return poly(COS, v), -u * poly(SIN, v)


def one_hot(condition):
    return jnp.where(condition, 1.0, 0.0).astype(BF16)


def total_wave(dest, k):
    t = (dest & 7) + 8 * k
    zz = (t * 205) >> 10
    return 20 * zz + 5 * (dest >> 3) + (t - 5 * zz)


def kernel(count_ref, wave_ref, waves_ref, field_ref, leg_ref, out_ref,
           fi, li, fm, tbl, base, xs, xg, zs0, zs1, zs2, zs3, zr0, zr1, zr2, zr3, xr, p256, pz, prow, pcol, lr, lu, lv, lul, lvl, lw,
           ps0, ps1, ps2, ps3, ps4, ps5, pr0, pr1, pr2, pr3, pr4, pr5, ab, mt, acc, rs, r1, r2s, r2,
           in_sem, zs_sem, zr_sem, xs_sem, xr_sem, ps_sem, pr_sem, r1s_sem, r1_sem, r2s_sem, r2_sem):
    field_in = pltpu.make_async_copy(field_ref, fi, in_sem.at[0])
    leg_in = pltpu.make_async_copy(leg_ref, li, in_sem.at[1])
    field_in.start()
    leg_in.start()
    lat = lax.axis_index("lat")
    d = lax.axis_index("mem")
    z, x = lat // X, lat % X
    me = x * D + d

    def z_partner(o):
        far = 8 - (o + 1) // 2
        other = (z + far + (1 - o % 2) * (Z - 2 * far)) % Z
        return other, (other * X + x, d)

    def plane_partner(step):
        other_x = (x + step[0]) % X
        other_d = (d // 2 + step[1]) % 4 * 2 + (d + step[2]) % 2
        return other_x * D + other_d, (z * X + other_x, other_d)

    barrier = pltpu.get_barrier_semaphore()

    for o in range(Z - 1):
        pl.semaphore_signal(barrier, inc=1, device_id=z_partner(o)[1], device_id_type=MESH)
    for o in range(1, X):
        pl.semaphore_signal(barrier, inc=1, device_id=(z * X + (x + o) % X, d), device_id_type=MESH)
    for o in range(1, D):
        pl.semaphore_signal(barrier, inc=1, device_id=(lat, (d + o) % D), device_id_type=MESH)

    count = count_ref[0].astype(F32)
    inverse = 1.0 / jnp.full((128, 128), count, F32)
    wave_row = waves_ref[...].astype(F32).reshape(1, M)
    p_row = iota((128, M), 0)

    def make_base(j, carry):
        slot = 10 * (4 * ((p_row >> 1) & 15) + (p_row >> 5)) + 2 * j + (p_row & 1)
        wave = jnp.sum(jnp.where(iota((128, M), 1) == slot, wave_row, 0.0), axis=1, keepdims=True)
        wave = jnp.broadcast_to(wave, (128, 128))
        c, s = unit(wave * iota((128, 128), 1).astype(F32), count, inverse)
        base[j, 0] = c
        base[j, 1] = s
        c, s = unit(wave * 128.0, count, inverse)
        base[j, 2] = c
        base[j, 3] = s
        return carry

    make_base(0, 0)
    field_in.wait()
    fm[...] = jnp.where(iota((LEV, LONS), 1) < count_ref[0], fi[...].astype(F32), 0.0).astype(BF16)

    def transform(j):
        def rows(b, inner):
            at = pl.ds(pl.multiple_of(b * 32, 32), 32)
            c, s = base[j, 0, at, :], base[j, 1, at, :]
            cw, sw = base[j, 2, at, :], base[j, 3, at, :]
            for a in range(LONS // 128):
                tbl[0, at, a * 128:(a + 1) * 128] = c.astype(BF16)
                tbl[1, at, a * 128:(a + 1) * 128] = s.astype(BF16)
                c, s = c * cw - s * sw, c * sw + s * cw
            return inner

        lax.fori_loop(0, 4, rows, 0)
        summed = dot(tbl[...].reshape(256, LONS), fm[...], 1, 1) / count
        for xx in range(X):
            at = xx * 32
            xs[j, xx] = jnp.concatenate([summed[at:at + 32], summed[128 + at:160 + at]], axis=0).astype(BF16)

    def send_x(j):
        xg[j, x] = xs[j, x]

        for o in range(1, X):
            other = (x + o) % X
            pltpu.make_async_remote_copy(
                src_ref=xs.at[j, other], dst_ref=xg.at[j, x], send_sem=xs_sem, recv_sem=xr_sem.at[j],
                device_id=(z * X + other, d), device_id_type=MESH).start()

    def pass_on(j, target, place):
        pltpu.make_async_copy(xg.at[j, 0:X - 1], xg.at[j, 0:X - 1], xr_sem.at[j]).wait()
        moved = dot(pz[...], xg[j].reshape(256, LEV), 1, 0).astype(BF16)
        target[:, place:place + 16, :] = moved.reshape(Z, 16, LEV)

    def send_z(stage, source, target):
        target[z] = source[z]

        for o in range(Z - 1):
            other, device = z_partner(o)
            pltpu.make_async_remote_copy(
                src_ref=source.at[other], dst_ref=target.at[z], send_sem=zs_sem.at[stage],
                recv_sem=zr_sem.at[stage], device_id=device, device_id_type=MESH).start()

    transform(0)
    pl.semaphore_wait(barrier, Z - 1 + X - 1 + D - 1)
    send_x(0)
    lax.fori_loop(1, PAIRS, make_base, 0)
    o_row, o_col = iota((256, 256), 0), iota((256, 256), 1)
    p256[...] = one_hot(o_col == (o_row & 15) * 16 + (o_row >> 4))
    pz[...] = one_hot(o_col == ((o_row >> 2) & 3) * 64 + ((o_row >> 1) & 1) * 32 + (o_row >> 4) * 2 + (o_row & 1))
    transform(1)
    send_x(1)
    pass_on(0, zs0, 0)
    send_z(0, zs0, zr0)
    transform(2)
    send_x(2)
    pass_on(1, zs1, 0)
    send_z(1, zs1, zr1)
    transform(3)
    send_x(3)
    transform(4)
    send_x(4)
    pass_on(2, zs2, 0)
    send_z(2, zs2, zr2)
    pass_on(3, zs3, 0)
    pass_on(4, zs3, 16)
    send_z(3, zs3, zr3)

    o_row, o_col = iota((128, 128), 0), iota((128, 128), 1)
    prow[...] = one_hot(o_col == ((o_row >> 4) & 1) * 64 + 4 * (o_row & 15) + (o_row >> 5))
    c_row = iota((256, 1), 0)
    i_main = total_wave(c_row >> 3, c_row & 7)
    i_left = total_wave(c_row >> 3, 8 + (c_row & 1))
    n_col = iota((256, M), 1)
    pcol[0:256] = one_hot(n_col == M - 1 - i_main)
    pcol[256:512] = one_hot(n_col == i_main)
    pcol[512:768] = one_hot(n_col == M - 1 - i_left)
    pcol[768:1024] = one_hot(n_col == i_left)

    lane_slot = (iota((1, 128), 1) >> 4) & 1
    left_j = (c_row >> 1) & 3

    def legendre(j):
        lr[j] = dot(prow[...], li[2 * j:2 * j + 2].reshape(128, M), 1, 0).astype(BF16)
        w0 = wave_ref[10 * lat + 2 * j]
        w1 = wave_ref[10 * lat + 2 * j + 1]
        low = jnp.minimum(w0, w1)
        small = jnp.where(lane_slot == 0, w0, w1) == low
        put = pcol[...]
        moved = dot(put, lr[j], 1, 1)
        upper, lower, upper_left, lower_left = (moved[a * 256:(a + 1) * 256] for a in range(4))
        high = jnp.where(small, upper, 0.0)
        deep = jnp.where(small, jnp.where(i_main >= low, lower, 0.0), jnp.where(i_main < low, upper, 0.0))
        if j >= 3:
            high, deep = high.reshape(GROUP, 8, 128), deep.reshape(GROUP, 8, 128)
            high, deep = (jnp.concatenate([high[:, a:a + 4], deep[:, a:a + 4]], axis=1).reshape(256, 128) for a in (0, 4))
        lu[j] = high.astype(BF16)
        lv[j] = deep.astype(BF16)
        here = left_j == j % 3
        lul[j] = jnp.where(here & small, upper_left, 0.0).astype(BF16)
        lvl[j] = jnp.where(small, jnp.where(here & (i_left >= low), lower_left, 0.0),
                           jnp.where(here & (i_left < low), upper_left, 0.0)).astype(BF16)
        pick = one_hot((iota((16, M), 0) == EXTRA[j]) & (iota((16, M), 1) == M - 1 - low))
        lw[j] = jnp.where(small, 0.0, dot(pick, lr[j], 1, 1)).astype(BF16)
        for xx in range(X):
            wave = wave_ref[10 * (X * z + xx) + 2 * j]
            mt[j, xx * 8:(xx + 1) * 8, :] = jnp.full((8, 128), jnp.minimum(wave, M - 1 - wave), jnp.int32)

    def rows_along_z(stage, source):
        pltpu.make_async_copy(source.at[0:Z - 1], source.at[0:Z - 1], zr_sem.at[stage]).wait()

    def gather(j, source, place):
        piece = source[:, place:place + 16, :].reshape(256, LEV)
        moved = dot(p256[...], piece, 1, 0).astype(BF16)
        for xx in range(X):
            for q in range(2):
                at = (xx * 4 + q * 2) * 16
                xr[j, xx, :, q * 128:(q + 1) * 128] = moved[at:at + 32]

    def both_kinds(up, low):
        return jnp.concatenate([up.reshape(GROUP, 8, 256), low.reshape(GROUP, 8, 256)], axis=1).astype(BF16)

    def spectral(j, target, place):
        rhs = xr[j].reshape(128, 256)
        target[:, place:place + 16, :] = both_kinds(dot(lu[j], rhs, 1, 0), dot(lv[j], rhs, 1, 0))

    def send_plane(stage, source, target):
        target[me] = source[me]

        for step in STEPS:
            other, device = plane_partner(step)
            pltpu.make_async_remote_copy(
                src_ref=source.at[other], dst_ref=target.at[me], send_sem=ps_sem.at[stage],
                recv_sem=pr_sem.at[stage], device_id=device, device_id_type=MESH).start()

    def left_over(js, target, place):
        up, low = jnp.zeros((256, 256), F32), jnp.zeros((256, 256), F32)
        extra = jnp.zeros((16, 256), F32)
        for j in js:
            rhs = xr[j].reshape(128, 256)
            up += dot(lul[j], rhs, 1, 0)
            low += dot(lvl[j], rhs, 1, 0)
            extra += dot(lw[j], rhs, 1, 0)
        up = up.reshape(GROUP, 8, 256) + extra[0:8][None]
        low = low.reshape(GROUP, 8, 256) + extra[8:16][None]
        target[:, place:place + 16, :] = both_kinds(up, low)

    leg_in.wait()
    legendre(0)
    rows_along_z(0, zr0)
    gather(0, zr0, 0)
    spectral(0, ps0, 0)
    send_plane(0, ps0, pr0)
    legendre(1)
    rows_along_z(1, zr1)
    gather(1, zr1, 0)
    spectral(1, ps1, 0)
    send_plane(1, ps1, pr1)
    legendre(2)
    rows_along_z(2, zr2)
    gather(2, zr2, 0)
    spectral(2, ps2, 0)
    left_over((0, 1, 2), ps2, 16)
    send_plane(2, ps2, pr2)
    legendre(3)
    legendre(4)

    def arrived(stage, target, subs, then=None):
        pltpu.make_async_copy(target.at[0:GROUP - 1], target.at[0:GROUP - 1], pr_sem.at[stage]).wait()
        if then is not None:
            send_plane(*then)
        for b, sub in enumerate(subs):
            for g in range(2):
                piece = target[g * 16:(g + 1) * 16, b * 16:(b + 1) * 16, :].reshape(256, 256)
                moved = dot(p256[...], piece, 1, 0).astype(BF16)
                ab[sub, :, g * 16:(g + 1) * 16, :] = moved.reshape(16, 16, 256)

    def halves(rows):
        return jnp.concatenate([rows[:, 0:128], rows[:, 128:256]], axis=0)

    def waves_of(js):
        tile = jnp.concatenate([mt[j] for j in js], axis=0)
        return jnp.concatenate([tile, tile], axis=0)

    def gram(k, ups, lows, js, first, extras=None, extra_js=()):
        i = total_wave(me, k)
        up = halves(jnp.concatenate(ups, axis=0))
        low = halves(jnp.concatenate(lows, axis=0))
        waves = waves_of(js)
        inside = low * one_hot(waves <= i)
        outside = low * one_hot(waves > i)
        near = dot(low, inside, 0, 0)
        far = dot(up, up, 0, 0) + dot(low, outside, 0, 0)
        if extras is not None:
            far += dot(extras, extras * one_hot(waves_of(extra_js) == i), 0, 0)
        if first:
            acc[k, 0] = near
            acc[k, 1] = far
        else:
            acc[k, 0] += near
            acc[k, 1] += far

    arrived(0, pr0, (0,))

    def gram_a(k, carry):
        gram(k, [ab[0, k]], [ab[0, 8 + k]], (0,), True)
        return carry

    lax.fori_loop(0, 8, gram_a, 0)

    rows_along_z(3, zr3)
    gather(3, zr3, 0)
    gather(4, zr3, 16)
    left_over((3, 4), ps3, 0)
    send_plane(3, ps3, pr3)
    rhs3, rhs4 = xr[3].reshape(128, 256), xr[4].reshape(128, 256)
    ps4[...] = both_kinds(dot(lu[3], rhs3, 1, 0), dot(lu[4], rhs4, 1, 0))
    send_plane(4, ps4, pr4)
    ps5[...] = both_kinds(dot(lv[3], rhs3, 1, 0), dot(lv[4], rhs4, 1, 0))

    arrived(1, pr1, (1,))
    arrived(2, pr2, (2, 5), (5, ps5, pr5))
    extras_b = halves(jnp.concatenate([ab[5, EXTRA[j]] for j in (0, 1, 2)], axis=0))

    def gram_b(k, carry):
        gram(k, [ab[1, k], ab[2, k]], [ab[1, 8 + k], ab[2, 8 + k]], (1, 2), False, extras_b, (0, 1, 2))
        return carry

    lax.fori_loop(0, 8, gram_b, 0)
    for kk in range(2):
        gram(8 + kk, [ab[5, 2 * j + kk] for j in range(3)], [ab[5, 8 + 2 * j + kk] for j in range(3)],
             (0, 1, 2), True, extras_b, (0, 1, 2))

    lane = iota((16, 128), 1)

    behind = 1 + d % 2

    def owner_of(k):
        return (d + 8 * k) // 5

    def toward(k):
        return (owner_of(k) - z + Z + behind) % 4 - behind

    def pack_send(k):
        for h in range(2):
            whole = acc[k, h]
            blocks = [whole[0:16]]
            for r in range(1, 4):
                folded = pltpu.roll(whole[16 * (8 - r):16 * (9 - r)], 16 * r, 1)
                blocks.append(jnp.where(lane >= 16 * r, whole[16 * r:16 * (r + 1)], folded))
            blocks.append(whole[64:80])
            rs[k, h * 80:(h + 1) * 80, :] = jnp.concatenate(blocks, axis=0).astype(BF16)
        step = toward(k)
        seat = step + behind

        @pl.when(step != 0)
        def _():
            pltpu.make_async_remote_copy(
                src_ref=rs.at[k], dst_ref=r1.at[k, seat - (seat + 3 - behind) // 4], send_sem=r1s_sem,
                recv_sem=r1_sem.at[k], device_id=(((z + step + Z) % Z) * X + x, d), device_id_type=MESH).start()

    keep = (iota((128, 128), 1) >> 4) >= (iota((128, 128), 0) >> 4)

    def level_two(k, carry):
        @pl.when(toward(k) == 0)
        def _():
            pltpu.make_async_copy(r1.at[k], r1.at[k], r1_sem.at[k]).wait()
            total = rs[k].astype(F32)
            for a in range(3):
                total += r1[k, a].astype(F32)
            for h in range(2):
                part = total[h * 80:(h + 1) * 80]
                blocks = [part[16 * r:16 * (r + 1)] for r in range(5)]
                for r in range(3, 0, -1):
                    blocks.append(pltpu.roll(part[16 * r:16 * (r + 1)], 128 - 16 * r, 1))
                upper = jnp.concatenate(blocks, axis=0)
                r2s[k, :, h] = jnp.where(keep, upper, upper.T).astype(BF16).reshape(D, 16, 128)
            owner = owner_of(k)
            seat = (d + 8 * k) % 5 * 4 + z // 4

            def send(o):
                other = (d + o) % D
                pltpu.make_async_remote_copy(
                    src_ref=r2s.at[k, other], dst_ref=r2.at[seat], send_sem=r2s_sem, recv_sem=r2_sem,
                    device_id=(owner * X + x, other), device_id_type=MESH).start()

            for o in range(1, D):
                send(o)

            @pl.when(owner == z)
            def _():
                r2[seat] = r2s[k, d]

            @pl.when(owner != z)
            def _():
                send(0)

        return carry

    arrived(3, pr3, (6,))
    extras_c = halves(jnp.concatenate([ab[6, EXTRA[j]] for j in (3, 4)], axis=0))

    def gram_left(kk, carry):
        gram(8 + kk, [ab[6, kk], ab[6, 2 + kk]], [ab[6, 8 + kk], ab[6, 10 + kk]], (3, 4), False, extras_c, (3, 4))
        pack_send(8 + kk)
        return carry

    lax.fori_loop(0, 2, gram_left, 0)
    for half, (source, sub) in enumerate(((pr4, 3), (pr5, 4))):
        arrived(4 + half, source, (sub,))

        def gram_c(k, carry, sub=sub, half=half):
            gram(4 * half + k, [ab[sub, k], ab[sub, 8 + k]], [ab[sub, 4 + k], ab[sub, 12 + k]], (3, 4), False,
                 extras_c, (3, 4))
            pack_send(4 * half + k)
            return carry

        lax.fori_loop(0, 4, gram_c, 0)
        if half == 0:
            lax.fori_loop(8, OWN, level_two, 0)

    lax.fori_loop(0, 4, level_two, 0)
    lax.fori_loop(4, 8, level_two, 0)
    holds = (d + 3 * z) % 8 < 5

    @pl.when(holds)
    def _():
        pltpu.make_async_copy(r2.at[0:19], r2.at[0:19], r2_sem).wait()

    @pl.when(jnp.logical_not(holds))
    def _():
        pltpu.make_async_copy(r2, r2, r2_sem).wait()

    for u in range(5):
        total = r2[4 * u].astype(F32)
        for a in range(1, 4):
            total += r2[4 * u + a].astype(F32)
        out_ref[:, u] = total * 0.125

    for stage, source in enumerate((zs0, zs1, zs2, zs3)):
        pltpu.make_async_copy(source.at[0:Z - 1], source.at[0:Z - 1], zs_sem.at[stage]).wait()
    for j in range(PAIRS):
        pltpu.make_async_copy(xs.at[j, 0:X - 1], xs.at[j, 0:X - 1], xs_sem).wait()
    for stage, source in enumerate((ps0, ps1, ps2, ps3, ps4, ps5)):
        pltpu.make_async_copy(source.at[0:GROUP - 1], source.at[0:GROUP - 1], ps_sem.at[stage]).wait()

    def sent(k, carry):
        @pl.when(toward(k) != 0)
        def _():
            pltpu.make_async_copy(rs.at[k], rs.at[k], r1s_sem).wait()

        @pl.when((toward(k) == 0) & (owner_of(k) != z))
        def _():
            pltpu.make_async_copy(r2s.at[k], r2s.at[k], r2s_sem).wait()

        @pl.when(owner_of(k) == z)
        def _():
            pltpu.make_async_copy(r2s.at[k, 0:D - 1], r2s.at[k, 0:D - 1], r2s_sem).wait()

        return carry

    lax.fori_loop(0, OWN, sent, 0)


def per_device(field, lon_count, wave_order, legendre):
    vmem = pl.BlockSpec(memory_space=pltpu.VMEM)
    smem = pl.BlockSpec(memory_space=pltpu.SMEM)
    V = pltpu.VMEM
    scratch = [
        V((LEV, LONS), BF16), V((2 * PAIRS, NLAT, M), BF16),
        V((LEV, LONS), BF16), V((2, 128, LONS), BF16), V((PAIRS, 4, 128, 128), F32),
        V((PAIRS, X, 64, LEV), BF16), V((PAIRS, X, 64, LEV), BF16),
        *[V((Z, rows, LEV), BF16) for rows in (16, 16, 16, 32)] * 2, V((PAIRS, X, 32, 256), BF16), V((256, 256), BF16),
        V((256, 256), BF16), V((128, 128), BF16), V((1024, M), BF16), V((PAIRS, 128, M), BF16),
        V((PAIRS, 256, 128), BF16), V((PAIRS, 256, 128), BF16),
        V((PAIRS, 256, 128), BF16), V((PAIRS, 256, 128), BF16), V((PAIRS, 16, 128), BF16),
        *[V((GROUP, rows, 256), BF16) for rows in (16, 16, 32, 16, 16, 16)] * 2,
        V((7, 16, GROUP, 256), BF16), V((PAIRS, 32, 128), jnp.int32), V((OWN, 2, 128, 128), F32),
        V((OWN, 160, 128), BF16), V((OWN, 3, 160, 128), BF16), V((OWN, D, 2, 16, 128), BF16),
        V((20, 2, 16, 128), BF16),
        pltpu.SemaphoreType.DMA((2,)),
        pltpu.SemaphoreType.DMA((4,)), pltpu.SemaphoreType.DMA((4,)),
        pltpu.SemaphoreType.DMA, pltpu.SemaphoreType.DMA((PAIRS,)),
        pltpu.SemaphoreType.DMA((6,)), pltpu.SemaphoreType.DMA((6,)),
        pltpu.SemaphoreType.DMA, pltpu.SemaphoreType.DMA((OWN,)),
        pltpu.SemaphoreType.DMA, pltpu.SemaphoreType.DMA,
    ]
    hbm = pl.BlockSpec(memory_space=pltpu.HBM)
    return pl.pallas_call(
        kernel,
        out_shape=jax.ShapeDtypeStruct((2, 5, 16, 128), F32),
        in_specs=[smem, smem, vmem, hbm, hbm],
        out_specs=vmem,
        scratch_shapes=scratch,
        compiler_params=pltpu.CompilerParams(
            collective_id=0, has_side_effects=True, vmem_limit_bytes=54784 * 1024),
    )(lon_count, wave_order, wave_order, field.reshape(LEV, LONS), legendre)


def solution(mesh):
    return jax.shard_map(
        per_device,
        mesh=mesh,
        in_specs=(P("mem", "lat", None, None), P("lat"), P(), P("lat", None, None)),
        out_specs=P(None, "lat", "mem", None),
        check_vma=False,
    )
```

```python
import jax
import jax.numpy as jnp
from jax import lax
from jax.experimental import pallas as pl
from jax.experimental.pallas import tpu as pltpu
from jax.sharding import PartitionSpec as P

MESH = pl.DeviceIdType.MESH
F32 = jnp.float32
BF16 = jnp.bfloat16
Z, X, D = 16, 4, 8
GROUP = X * D
LEV, LONS, M, NLAT = 128, 2688, 640, 64
PAIRS = 5
EXTRA = (6, 7, 14, 4, 5)
OWN = 10
COS = (1.0, -19.739208221435547, 64.93939208984375, -85.45681762695312, 60.24457931518555,
       -26.425565719604492, 7.898900985717773, -1.6961979866027832, 0.24304766952991486)
SIN = (6.2831854820251465, -41.34170150756836, 81.6052474975586, -76.70585632324219, 42.05867385864258,
       -15.094411849975586, 3.818404197692871, -0.7120527029037476, 0.09126123040914536)


STEPS = sorted(((dx, dy, dc) for dx in range(4) for dy in range(4) for dc in range(2) if dx or dy or dc),
               key=lambda s: (11 * (s[0] * 8 + s[1] * 2 + s[2])) % 32)


def iota(shape, dim):
    return lax.broadcasted_iota(jnp.int32, shape, dim)


def dot(a, b, ca, cb):
    return lax.dot_general(a, b, (((ca,), (cb,)), ((), ())), preferred_element_type=F32)


def poly(coefficients, v):
    total = jnp.full_like(v, coefficients[-1])
    for value in coefficients[-2::-1]:
        total = total * v + value
    return total


def unit(product, count, inverse):
    turns = jnp.floor(product * inverse + 0.5)
    u = (product - turns * count) * inverse
    v = u * u
    return poly(COS, v), -u * poly(SIN, v)


def one_hot(condition):
    return jnp.where(condition, 1.0, 0.0).astype(BF16)


def total_wave(dest, k):
    t = (dest & 7) + 8 * k
    zz = (t * 205) >> 10
    return 20 * zz + 5 * (dest >> 3) + (t - 5 * zz)


def kernel(count_ref, wave_ref, waves_ref, field_ref, leg_ref, out_ref,
           fi, li, fm, tbl, base, xs, xg, zs0, zs1, zs2, zs3, zr0, zr1, zr2, zr3, xr, p256, pz, prow, pcol, lr, lu, lv, lul, lvl, lw,
           ps0, ps1, ps2, ps3, ps4, ps5, pr0, pr1, pr2, pr3, pr4, pr5, ab, mt, acc, rs, r1, r2s, r2,
           in_sem, zs_sem, zr_sem, xs_sem, xr_sem, ps_sem, pr_sem, r1s_sem, r1_sem, r2s_sem, r2_sem):
    field_in = pltpu.make_async_copy(field_ref, fi, in_sem.at[0])
    leg_in = pltpu.make_async_copy(leg_ref, li, in_sem.at[1])
    field_in.start()
    leg_in.start()
    lat = lax.axis_index("lat")
    d = lax.axis_index("mem")
    z, x = lat // X, lat % X
    me = x * D + d

    def z_partner(o):
        far = 8 - (o + 1) // 2
        other = (z + far + (1 - o % 2) * (Z - 2 * far)) % Z
        return other, (other * X + x, d)

    def plane_partner(step):
        other_x = (x + step[0]) % X
        other_d = (d // 2 + step[1]) % 4 * 2 + (d + step[2]) % 2
        return other_x * D + other_d, (z * X + other_x, other_d)

    barrier = pltpu.get_barrier_semaphore()

    for o in range(Z - 1):
        pl.semaphore_signal(barrier, inc=1, device_id=z_partner(o)[1], device_id_type=MESH)
    for o in range(1, X):
        pl.semaphore_signal(barrier, inc=1, device_id=(z * X + (x + o) % X, d), device_id_type=MESH)
    for o in range(1, D):
        pl.semaphore_signal(barrier, inc=1, device_id=(lat, (d + o) % D), device_id_type=MESH)

    count = count_ref[0].astype(F32)
    inverse = 1.0 / jnp.full((128, 128), count, F32)
    wave_row = waves_ref[...].astype(F32).reshape(1, M)
    p_row = iota((128, M), 0)

    def make_base(j, carry):
        slot = 10 * (4 * ((p_row >> 1) & 15) + (p_row >> 5)) + 2 * j + (p_row & 1)
        wave = jnp.sum(jnp.where(iota((128, M), 1) == slot, wave_row, 0.0), axis=1, keepdims=True)
        wave = jnp.broadcast_to(wave, (128, 128))
        c, s = unit(wave * iota((128, 128), 1).astype(F32), count, inverse)
        base[j, 0] = c
        base[j, 1] = s
        c, s = unit(wave * 128.0, count, inverse)
        base[j, 2] = c
        base[j, 3] = s
        return carry

    make_base(0, 0)
    field_in.wait()
    fm[...] = jnp.where(iota((LEV, LONS), 1) < count_ref[0], fi[...].astype(F32), 0.0).astype(BF16)

    def transform(j):
        def rows(b, inner):
            at = pl.ds(pl.multiple_of(b * 32, 32), 32)
            c, s = base[j, 0, at, :], base[j, 1, at, :]
            cw, sw = base[j, 2, at, :], base[j, 3, at, :]
            for a in range(LONS // 128):
                tbl[0, at, a * 128:(a + 1) * 128] = c.astype(BF16)
                tbl[1, at, a * 128:(a + 1) * 128] = s.astype(BF16)
                c, s = c * cw - s * sw, c * sw + s * cw
            return inner

        lax.fori_loop(0, 4, rows, 0)
        summed = dot(tbl[...].reshape(256, LONS), fm[...], 1, 1) / count
        for xx in range(X):
            at = xx * 32
            xs[j, xx] = jnp.concatenate([summed[at:at + 32], summed[128 + at:160 + at]], axis=0).astype(BF16)

    def send_x(j):
        xg[j, x] = xs[j, x]

        for o in range(1, X):
            other = (x + o) % X
            pltpu.make_async_remote_copy(
                src_ref=xs.at[j, other], dst_ref=xg.at[j, x], send_sem=xs_sem, recv_sem=xr_sem.at[j],
                device_id=(z * X + other, d), device_id_type=MESH).start()

    def pass_on(j, target, place):
        pltpu.make_async_copy(xg.at[j, 0:X - 1], xg.at[j, 0:X - 1], xr_sem.at[j]).wait()
        moved = dot(pz[...], xg[j].reshape(256, LEV), 1, 0).astype(BF16)
        target[:, place:place + 16, :] = moved.reshape(Z, 16, LEV)

    def send_z(stage, source, target):
        target[z] = source[z]

        for o in range(Z - 1):
            other, device = z_partner(o)
            pltpu.make_async_remote_copy(
                src_ref=source.at[other], dst_ref=target.at[z], send_sem=zs_sem.at[stage],
                recv_sem=zr_sem.at[stage], device_id=device, device_id_type=MESH).start()

    transform(0)
    pl.semaphore_wait(barrier, Z - 1 + X - 1 + D - 1)
    send_x(0)
    lax.fori_loop(1, PAIRS, make_base, 0)
    o_row, o_col = iota((256, 256), 0), iota((256, 256), 1)
    p256[...] = one_hot(o_col == (o_row & 15) * 16 + (o_row >> 4))
    pz[...] = one_hot(o_col == ((o_row >> 2) & 3) * 64 + ((o_row >> 1) & 1) * 32 + (o_row >> 4) * 2 + (o_row & 1))
    transform(1)
    send_x(1)
    pass_on(0, zs0, 0)
    send_z(0, zs0, zr0)
    transform(2)
    send_x(2)
    pass_on(1, zs1, 0)
    send_z(1, zs1, zr1)
    transform(3)
    send_x(3)
    transform(4)
    send_x(4)
    pass_on(2, zs2, 0)
    send_z(2, zs2, zr2)
    pass_on(3, zs3, 0)
    pass_on(4, zs3, 16)
    send_z(3, zs3, zr3)

    o_row, o_col = iota((128, 128), 0), iota((128, 128), 1)
    prow[...] = one_hot(o_col == ((o_row >> 4) & 1) * 64 + 4 * (o_row & 15) + (o_row >> 5))
    c_row = iota((256, 1), 0)
    i_main = total_wave(c_row >> 3, c_row & 7)
    i_left = total_wave(c_row >> 3, 8 + (c_row & 1))
    n_col = iota((256, M), 1)
    pcol[0:256] = one_hot(n_col == M - 1 - i_main)
    pcol[256:512] = one_hot(n_col == i_main)
    pcol[512:768] = one_hot(n_col == M - 1 - i_left)
    pcol[768:1024] = one_hot(n_col == i_left)

    lane_slot = (iota((1, 128), 1) >> 4) & 1
    left_j = (c_row >> 1) & 3

    def legendre(j):
        lr[j] = dot(prow[...], li[2 * j:2 * j + 2].reshape(128, M), 1, 0).astype(BF16)
        w0 = wave_ref[10 * lat + 2 * j]
        w1 = wave_ref[10 * lat + 2 * j + 1]
        low = jnp.minimum(w0, w1)
        small = jnp.where(lane_slot == 0, w0, w1) == low
        put = pcol[...]
        moved = dot(put, lr[j], 1, 1)
        upper, lower, upper_left, lower_left = (moved[a * 256:(a + 1) * 256] for a in range(4))
        high = jnp.where(small, upper, 0.0)
        deep = jnp.where(small, jnp.where(i_main >= low, lower, 0.0), jnp.where(i_main < low, upper, 0.0))
        if j >= 3:
            high, deep = high.reshape(GROUP, 8, 128), deep.reshape(GROUP, 8, 128)
            high, deep = (jnp.concatenate([high[:, a:a + 4], deep[:, a:a + 4]], axis=1).reshape(256, 128) for a in (0, 4))
        lu[j] = high.astype(BF16)
        lv[j] = deep.astype(BF16)
        here = left_j == j % 3
        lul[j] = jnp.where(here & small, upper_left, 0.0).astype(BF16)
        lvl[j] = jnp.where(small, jnp.where(here & (i_left >= low), lower_left, 0.0),
                           jnp.where(here & (i_left < low), upper_left, 0.0)).astype(BF16)
        pick = one_hot((iota((16, M), 0) == EXTRA[j]) & (iota((16, M), 1) == M - 1 - low))
        lw[j] = jnp.where(small, 0.0, dot(pick, lr[j], 1, 1)).astype(BF16)
        for xx in range(X):
            wave = wave_ref[10 * (X * z + xx) + 2 * j]
            mt[j, xx * 8:(xx + 1) * 8, :] = jnp.full((8, 128), jnp.minimum(wave, M - 1 - wave), jnp.int32)

    def rows_along_z(stage, source):
        pltpu.make_async_copy(source.at[0:Z - 1], source.at[0:Z - 1], zr_sem.at[stage]).wait()

    def gather(j, source, place):
        piece = source[:, place:place + 16, :].reshape(256, LEV)
        moved = dot(p256[...], piece, 1, 0).astype(BF16)
        for xx in range(X):
            for q in range(2):
                at = (xx * 4 + q * 2) * 16
                xr[j, xx, :, q * 128:(q + 1) * 128] = moved[at:at + 32]

    def both_kinds(up, low):
        return jnp.concatenate([up.reshape(GROUP, 8, 256), low.reshape(GROUP, 8, 256)], axis=1).astype(BF16)

    def spectral(j, target, place):
        rhs = xr[j].reshape(128, 256)
        target[:, place:place + 16, :] = both_kinds(dot(lu[j], rhs, 1, 0), dot(lv[j], rhs, 1, 0))

    def send_plane(stage, source, target):
        target[me] = source[me]

        for step in STEPS:
            other, device = plane_partner(step)
            pltpu.make_async_remote_copy(
                src_ref=source.at[other], dst_ref=target.at[me], send_sem=ps_sem.at[stage],
                recv_sem=pr_sem.at[stage], device_id=device, device_id_type=MESH).start()

    def left_over(js, target, place):
        up, low = jnp.zeros((256, 256), F32), jnp.zeros((256, 256), F32)
        extra = jnp.zeros((16, 256), F32)
        for j in js:
            rhs = xr[j].reshape(128, 256)
            up += dot(lul[j], rhs, 1, 0)
            low += dot(lvl[j], rhs, 1, 0)
            extra += dot(lw[j], rhs, 1, 0)
        up = up.reshape(GROUP, 8, 256) + extra[0:8][None]
        low = low.reshape(GROUP, 8, 256) + extra[8:16][None]
        target[:, place:place + 16, :] = both_kinds(up, low)

    leg_in.wait()
    legendre(0)
    rows_along_z(0, zr0)
    gather(0, zr0, 0)
    spectral(0, ps0, 0)
    send_plane(0, ps0, pr0)
    legendre(1)
    rows_along_z(1, zr1)
    gather(1, zr1, 0)
    spectral(1, ps1, 0)
    send_plane(1, ps1, pr1)
    legendre(2)
    rows_along_z(2, zr2)
    gather(2, zr2, 0)
    spectral(2, ps2, 0)
    left_over((0, 1, 2), ps2, 16)
    send_plane(2, ps2, pr2)
    legendre(3)
    legendre(4)

    def arrived(stage, target, subs, then=None):
        pltpu.make_async_copy(target.at[0:GROUP - 1], target.at[0:GROUP - 1], pr_sem.at[stage]).wait()
        if then is not None:
            send_plane(*then)
        for b, sub in enumerate(subs):
            for g in range(2):
                piece = target[g * 16:(g + 1) * 16, b * 16:(b + 1) * 16, :].reshape(256, 256)
                moved = dot(p256[...], piece, 1, 0).astype(BF16)
                ab[sub, :, g * 16:(g + 1) * 16, :] = moved.reshape(16, 16, 256)

    def halves(rows):
        return jnp.concatenate([rows[:, 0:128], rows[:, 128:256]], axis=0)

    def waves_of(js):
        tile = jnp.concatenate([mt[j] for j in js], axis=0)
        return jnp.concatenate([tile, tile], axis=0)

    def gram(k, ups, lows, js, first, extras=None, extra_js=()):
        i = total_wave(me, k)
        up = halves(jnp.concatenate(ups, axis=0))
        low = halves(jnp.concatenate(lows, axis=0))
        waves = waves_of(js)
        inside = low * one_hot(waves <= i)
        outside = low * one_hot(waves > i)
        near = dot(low, inside, 0, 0)
        far = dot(up, up, 0, 0) + dot(low, outside, 0, 0)
        if extras is not None:
            far += dot(extras, extras * one_hot(waves_of(extra_js) == i), 0, 0)
        if first:
            acc[k, 0] = near
            acc[k, 1] = far
        else:
            acc[k, 0] += near
            acc[k, 1] += far

    rows_along_z(3, zr3)
    gather(3, zr3, 0)
    gather(4, zr3, 16)
    left_over((3, 4), ps3, 0)
    send_plane(3, ps3, pr3)
    rhs3, rhs4 = xr[3].reshape(128, 256), xr[4].reshape(128, 256)
    ps4[...] = both_kinds(dot(lu[3], rhs3, 1, 0), dot(lu[4], rhs4, 1, 0))
    send_plane(4, ps4, pr4)
    ps5[...] = both_kinds(dot(lv[3], rhs3, 1, 0), dot(lv[4], rhs4, 1, 0))

    arrived(0, pr0, (0,))

    def gram_a(k, carry):
        gram(k, [ab[0, k]], [ab[0, 8 + k]], (0,), True)
        return carry

    lax.fori_loop(0, 8, gram_a, 0)

    arrived(1, pr1, (1,))
    arrived(2, pr2, (2, 5), (5, ps5, pr5))
    extras_b = halves(jnp.concatenate([ab[5, EXTRA[j]] for j in (0, 1, 2)], axis=0))

    def gram_b(k, carry):
        gram(k, [ab[1, k], ab[2, k]], [ab[1, 8 + k], ab[2, 8 + k]], (1, 2), False, extras_b, (0, 1, 2))
        return carry

    lax.fori_loop(0, 8, gram_b, 0)
    for kk in range(2):
        gram(8 + kk, [ab[5, 2 * j + kk] for j in range(3)], [ab[5, 8 + 2 * j + kk] for j in range(3)],
             (0, 1, 2), True, extras_b, (0, 1, 2))

    lane = iota((16, 128), 1)

    behind = 1 + d % 2

    def owner_of(k):
        return (d + 8 * k) // 5

    def toward(k):
        return (owner_of(k) - z + Z + behind) % 4 - behind

    def pack_send(k):
        for h in range(2):
            whole = acc[k, h]
            blocks = [whole[0:16]]
            for r in range(1, 4):
                folded = pltpu.roll(whole[16 * (8 - r):16 * (9 - r)], 16 * r, 1)
                blocks.append(jnp.where(lane >= 16 * r, whole[16 * r:16 * (r + 1)], folded))
            blocks.append(whole[64:80])
            rs[k, h * 80:(h + 1) * 80, :] = jnp.concatenate(blocks, axis=0).astype(BF16)
        step = toward(k)
        seat = step + behind

        @pl.when(step != 0)
        def _():
            pltpu.make_async_remote_copy(
                src_ref=rs.at[k], dst_ref=r1.at[k, seat - (seat + 3 - behind) // 4], send_sem=r1s_sem,
                recv_sem=r1_sem.at[k], device_id=(((z + step + Z) % Z) * X + x, d), device_id_type=MESH).start()

    keep = (iota((128, 128), 1) >> 4) >= (iota((128, 128), 0) >> 4)

    def level_two(k, carry):
        @pl.when(toward(k) == 0)
        def _():
            pltpu.make_async_copy(r1.at[k], r1.at[k], r1_sem.at[k]).wait()
            total = rs[k].astype(F32)
            for a in range(3):
                total += r1[k, a].astype(F32)
            for h in range(2):
                part = total[h * 80:(h + 1) * 80]
                blocks = [part[16 * r:16 * (r + 1)] for r in range(5)]
                for r in range(3, 0, -1):
                    blocks.append(pltpu.roll(part[16 * r:16 * (r + 1)], 128 - 16 * r, 1))
                upper = jnp.concatenate(blocks, axis=0)
                r2s[k, :, h] = jnp.where(keep, upper, upper.T).astype(BF16).reshape(D, 16, 128)
            owner = owner_of(k)
            seat = (d + 8 * k) % 5 * 4 + z // 4

            def send(o):
                other = (d + o) % D
                pltpu.make_async_remote_copy(
                    src_ref=r2s.at[k, other], dst_ref=r2.at[seat], send_sem=r2s_sem, recv_sem=r2_sem,
                    device_id=(owner * X + x, other), device_id_type=MESH).start()

            for o in range(1, D):
                send(o)

            @pl.when(owner == z)
            def _():
                r2[seat] = r2s[k, d]

            @pl.when(owner != z)
            def _():
                send(0)

        return carry

    arrived(3, pr3, (6,))
    extras_c = halves(jnp.concatenate([ab[6, EXTRA[j]] for j in (3, 4)], axis=0))

    def gram_left(kk, carry):
        gram(8 + kk, [ab[6, kk], ab[6, 2 + kk]], [ab[6, 8 + kk], ab[6, 10 + kk]], (3, 4), False, extras_c, (3, 4))
        pack_send(8 + kk)
        return carry

    lax.fori_loop(0, 2, gram_left, 0)
    for half, (source, sub) in enumerate(((pr4, 3), (pr5, 4))):
        arrived(4 + half, source, (sub,))

        def gram_c(k, carry, sub=sub, half=half):
            gram(4 * half + k, [ab[sub, k], ab[sub, 8 + k]], [ab[sub, 4 + k], ab[sub, 12 + k]], (3, 4), False,
                 extras_c, (3, 4))
            pack_send(4 * half + k)
            return carry

        lax.fori_loop(0, 4, gram_c, 0)
        if half == 0:
            lax.fori_loop(8, OWN, level_two, 0)

    lax.fori_loop(0, 4, level_two, 0)
    lax.fori_loop(4, 8, level_two, 0)
    holds = (d + 3 * z) % 8 < 5

    @pl.when(holds)
    def _():
        pltpu.make_async_copy(r2.at[0:19], r2.at[0:19], r2_sem).wait()

    @pl.when(jnp.logical_not(holds))
    def _():
        pltpu.make_async_copy(r2, r2, r2_sem).wait()

    for u in range(5):
        total = r2[4 * u].astype(F32)
        for a in range(1, 4):
            total += r2[4 * u + a].astype(F32)
        out_ref[:, u] = total * 0.125

    for stage, source in enumerate((zs0, zs1, zs2, zs3)):
        pltpu.make_async_copy(source.at[0:Z - 1], source.at[0:Z - 1], zs_sem.at[stage]).wait()
    for j in range(PAIRS):
        pltpu.make_async_copy(xs.at[j, 0:X - 1], xs.at[j, 0:X - 1], xs_sem).wait()
    for stage, source in enumerate((ps0, ps1, ps2, ps3, ps4, ps5)):
        pltpu.make_async_copy(source.at[0:GROUP - 1], source.at[0:GROUP - 1], ps_sem.at[stage]).wait()

    def sent(k, carry):
        @pl.when(toward(k) != 0)
        def _():
            pltpu.make_async_copy(rs.at[k], rs.at[k], r1s_sem).wait()

        @pl.when((toward(k) == 0) & (owner_of(k) != z))
        def _():
            pltpu.make_async_copy(r2s.at[k], r2s.at[k], r2s_sem).wait()

        @pl.when(owner_of(k) == z)
        def _():
            pltpu.make_async_copy(r2s.at[k, 0:D - 1], r2s.at[k, 0:D - 1], r2s_sem).wait()

        return carry

    lax.fori_loop(0, OWN, sent, 0)


def per_device(field, lon_count, wave_order, legendre):
    vmem = pl.BlockSpec(memory_space=pltpu.VMEM)
    smem = pl.BlockSpec(memory_space=pltpu.SMEM)
    V = pltpu.VMEM
    scratch = [
        V((LEV, LONS), BF16), V((2 * PAIRS, NLAT, M), BF16),
        V((LEV, LONS), BF16), V((2, 128, LONS), BF16), V((PAIRS, 4, 128, 128), F32),
        V((PAIRS, X, 64, LEV), BF16), V((PAIRS, X, 64, LEV), BF16),
        *[V((Z, rows, LEV), BF16) for rows in (16, 16, 16, 32)] * 2, V((PAIRS, X, 32, 256), BF16), V((256, 256), BF16),
        V((256, 256), BF16), V((128, 128), BF16), V((1024, M), BF16), V((PAIRS, 128, M), BF16),
        V((PAIRS, 256, 128), BF16), V((PAIRS, 256, 128), BF16),
        V((PAIRS, 256, 128), BF16), V((PAIRS, 256, 128), BF16), V((PAIRS, 16, 128), BF16),
        *[V((GROUP, rows, 256), BF16) for rows in (16, 16, 32, 16, 16, 16)] * 2,
        V((7, 16, GROUP, 256), BF16), V((PAIRS, 32, 128), jnp.int32), V((OWN, 2, 128, 128), F32),
        V((OWN, 160, 128), BF16), V((OWN, 3, 160, 128), BF16), V((OWN, D, 2, 16, 128), BF16),
        V((20, 2, 16, 128), BF16),
        pltpu.SemaphoreType.DMA((2,)),
        pltpu.SemaphoreType.DMA((4,)), pltpu.SemaphoreType.DMA((4,)),
        pltpu.SemaphoreType.DMA, pltpu.SemaphoreType.DMA((PAIRS,)),
        pltpu.SemaphoreType.DMA((6,)), pltpu.SemaphoreType.DMA((6,)),
        pltpu.SemaphoreType.DMA, pltpu.SemaphoreType.DMA((OWN,)),
        pltpu.SemaphoreType.DMA, pltpu.SemaphoreType.DMA,
    ]
    hbm = pl.BlockSpec(memory_space=pltpu.HBM)
    return pl.pallas_call(
        kernel,
        out_shape=jax.ShapeDtypeStruct((2, 5, 16, 128), F32),
        in_specs=[smem, smem, vmem, hbm, hbm],
        out_specs=vmem,
        scratch_shapes=scratch,
        compiler_params=pltpu.CompilerParams(
            collective_id=0, has_side_effects=True, vmem_limit_bytes=54784 * 1024),
    )(lon_count, wave_order, wave_order, field.reshape(LEV, LONS), legendre)


def solution(mesh):
    return jax.shard_map(
        per_device,
        mesh=mesh,
        in_specs=(P("mem", "lat", None, None), P("lat"), P(), P("lat", None, None)),
        out_specs=P(None, "lat", "mem", None),
        check_vma=False,
    )
```
